32 devices in a mesh: rows: 8 (over y, x, core), cols: 4 (over z).
Axes of the slice: x: 2, y: 2, z: 4, core: 2. Of those that a mesh axis runs over, the one named last changes fastest.
Arguments:
- points: float32 [4096, 256], P('rows'), may hold values from -4 to 4, as said below
- centers: float32 [16384, 256], P('cols'), may hold values from -4 to 4, as said below
- inv_factor: float32 [16384, 16384], P('cols', 'rows'), may hold values from -2 to 2, as said below
- solution: float32 [16384, 128], P('rows'), may hold values from -6 to 6
- residual: float32 [16384, 128], P('rows'), may hold values from -40 to 40
- direction: float32 [16384, 128], P('rows'), may hold values from -40 to 40
Outputs:
- new_solution: float32 [16384, 128], P('rows')
- new_residual: float32 [16384, 128], P('rows')
- new_direction: float32 [16384, 128], P('rows')
The draws below stay inside these ranges and needn't reach their ends.
Inputs may be any that keep to these rules, and one draw needn't show every extreme that they name: `points`: each point's coordinates have a fixed spread that differs from coordinate to coordinate. `centers`: drawn by the same law as points. `inv_factor`: upper triangular with a positive diagonal.
All inputs are finite; a program needn't handle non-finite values.
Results may differ from the reference program's by a relative error of at most 0.00027.
Values sent between devices are 32-bit elements; how exact they have to be, the bound alone decides.
No kernel may reach another device: no remote copies, remote signals or barrier semaphores. Data moves between devices by JAX's collectives and lax.ppermute only.
A program may use at most 128 MiB of HBM per device.

```python
import math
import jax
import jax.numpy as jnp
from jax import lax

D = 256
CENTERS = 16384
TARGETS = 128
ROWS_DEV = 512
POINTS = 4096
N_ROWS = 8


def spectrum_points(key, count):
    scales = jnp.sqrt(0.83 / (jnp.arange(D, dtype=jnp.float32) + 1.0))
    values = jnp.clip(jax.random.normal(key, (count, D), jnp.float32), -4.0, 4.0)
    return values * scales[None, :]


def draw_points(key, part):
    return spectrum_points(jax.random.fold_in(key, 11), POINTS)


def draw_centers(key, part):
    return spectrum_points(jax.random.fold_in(key, 23), CENTERS)


def draw_inv_factor(key, part):
    first_key, second_key = jax.random.split(jax.random.fold_in(key, 37))
    level = math.sqrt(250.0 / math.sqrt(POINTS * CENTERS))
    diagonal = level * jnp.exp(jax.random.uniform(first_key, (CENTERS,), jnp.float32, math.log(0.5), math.log(2.0)))
    upper_part = jnp.clip(jax.random.normal(second_key, (CENTERS, CENTERS), jnp.float32), -4.0, 4.0)
    upper_part = upper_part * (level / math.sqrt(CENTERS))
    return jnp.triu(upper_part, 1) + jnp.diag(diagonal)


def scaled_vector(key):
    first_key, second_key = jax.random.split(key, 2)
    row_scale = 0.3 * jnp.power(10.0, jnp.arange(CENTERS, dtype=jnp.float32) / CENTERS)
    col_scale = jnp.exp(jax.random.uniform(second_key, (TARGETS,), jnp.float32, math.log(0.3), math.log(3.0)))
    values = jnp.clip(jax.random.normal(first_key, (CENTERS, TARGETS), jnp.float32), -4.0, 4.0)
    return values * row_scale[:, None] * col_scale[None, :]


def draw_residual(key, part):
    return scaled_vector(jax.random.fold_in(key, 31))


def draw_direction(key, part):
    return scaled_vector(jax.random.fold_in(key, 47))


def level_of(own_key, extent, cuts, smallest, top_value):
    loudness, own = 1.0, jax.random.fold_in(own_key, 6)
    for position, parts in cuts:
        draws = jnp.exp(jax.random.uniform(jax.random.fold_in(own, position), (parts,), jnp.float32, smallest / len(cuts), top_value / len(cuts)))
        loudness = loudness * jnp.repeat(draws, extent[position] // parts).reshape([-1 if axis == position else 1 for axis in range(len(extent))])
    return loudness


def centred(rng, shape, scale, most, cuts=(), kind=jnp.bfloat16):
    result = scale * jax.random.normal(rng, shape, jnp.float32)
    if cuts:
        result = result * level_of(rng, shape, cuts, -0.22, 0.18)
    return jnp.clip(result, -most, most).astype(kind)


def setup_inputs(seed: int = 0) -> dict:
    seeds = jax.random.split(jax.random.key(seed), 7)
    return {
        "points": draw_points(jax.random.fold_in(seeds[6], 71), 0),
        "centers": draw_centers(jax.random.fold_in(seeds[6], 71), 0),
        "inv_factor": draw_inv_factor(jax.random.fold_in(seeds[6], 71), 0),
        "solution": centred(seeds[3], (CENTERS, TARGETS), 1.0, 6.0, ((0, 8),), jnp.float32),
        "residual": draw_residual(jax.random.fold_in(seeds[6], 71), 0),
        "direction": draw_direction(jax.random.fold_in(seeds[6], 71), 0),
    }


ridge_weight = 0.02


def reference(points, centers, inv_factor, solution, residual, direction):
    highest = lax.Precision.HIGHEST
    mapped = jnp.dot(inv_factor, direction, precision=highest, preferred_element_type=jnp.float32)
    center_sq = jnp.sum(centers * centers, axis=1)
    blocks = points.reshape(N_ROWS, ROWS_DEV, D)

    def add_block(accumulated, point_block):
        point_sq = jnp.sum(point_block * point_block, axis=1)
        inner_products = lax.dot_general(point_block, centers, (((1,), (1,)), ((), ())), precision=highest, preferred_element_type=jnp.float32)
        kernel = jnp.exp(-0.5 * ((point_sq[:, None] + center_sq[None, :]) - 2.0 * inner_products))
        predicted = jnp.dot(kernel, mapped, precision=highest, preferred_element_type=jnp.float32)
        back_part = lax.dot_general(kernel, predicted, (((0,), (0,)), ((), ())), precision=highest, preferred_element_type=jnp.float32)
        return accumulated + back_part, None

    back, unused = lax.scan(add_block, jnp.zeros((CENTERS, TARGETS), jnp.float32), blocks)
    image = lax.dot_general(inv_factor, back, (((0,), (0,)), ((), ())), precision=highest, preferred_element_type=jnp.float32) + ridge_weight * direction
    norm_now = jnp.sum(residual * residual, axis=0)
    curvature = jnp.sum(direction * image, axis=0)
    step_size = norm_now / curvature
    new_solution = solution + step_size[None, :] * direction
    new_residual = residual - step_size[None, :] * image
    norm_next = jnp.sum(new_residual * new_residual, axis=0)
    new_direction = new_residual + (norm_next / norm_now)[None, :] * direction
    return new_solution, new_residual, new_direction
```

```python
import functools

import jax
import jax.numpy as jnp
from jax import lax
from jax.experimental import pallas as pl
from jax.experimental.pallas import tpu as pltpu
from jax.sharding import PartitionSpec as P

ridge_weight = 0.02
PAD = 8
f32, bf16 = jnp.float32, jnp.bfloat16
FIRST = (((0,), (0,)), ((), ()))
LAST = (((1,), (1,)), ((), ()))


def split(value):
    high = value.astype(bf16)
    return high, (value - high.astype(f32)).astype(bf16)


def pair(value):
    high, low = split(value)
    return jnp.concatenate([high, low], axis=1)


def wide(lhs, pairs, dims=None):
    high, low = split(lhs)
    n = pairs.shape[1] // 2
    both = jnp.dot(high, pairs, preferred_element_type=f32)
    both += jnp.dot(low, pairs, preferred_element_type=f32)
    return both[:, :n] + both[:, n:]


def turned(pairs, high, low):
    n = pairs.shape[1] // 2
    both = lax.dot_general(pairs, high, FIRST, preferred_element_type=f32)
    both += lax.dot_general(pairs, low, FIRST, preferred_element_type=f32)
    return both[:n] + both[n:]


def params(mib=56):
    return pltpu.CompilerParams(vmem_limit_bytes=mib << 20)


def cost(flops, nbytes, exps=0):
    return pl.CostEstimate(flops=flops, bytes_accessed=nbytes, transcendentals=exps)


def whole(shape):
    return pl.BlockSpec(shape, lambda *_: (0,) * len(shape))


def forward_kernel(place, l_ref, d_ref, r_ref, keep_ref, send_ref, pairs, norms):
    @pl.when(pl.program_id(0) == 0)
    def _():
        d, r = d_ref[...], r_ref[...]
        pairs[...] = pair(d)
        norms[...] = jnp.zeros_like(norms)
        norms[0:1, :] = jnp.sum(r * r, axis=0, keepdims=True)
        norms[1:2, :] = jnp.sum(d * d, axis=0, keepdims=True)

    m = l_ref.shape[0] // 2
    core = place[1]
    for out_ref, side in ((keep_ref, core), (send_ref, 1 - core)):
        rows = l_ref[pl.ds(pl.multiple_of(side * m, m), m), :]
        out_ref[0, :m, :] = wide(rows, pairs[...])
        out_ref[0, m:, :] = norms[...]


def forward(place, inv_factor, direction, residual, chips):
    n, depth = inv_factor.shape
    t = direction.shape[1]
    m = n // chips // 2
    out = jax.ShapeDtypeStruct((chips, m + PAD, t), f32)
    block = pl.BlockSpec((1, m + PAD, t), lambda i, s: (i, 0, 0))
    return pl.pallas_call(
        forward_kernel,
        grid_spec=pltpu.PrefetchScalarGridSpec(
            num_scalar_prefetch=1,
            grid=(chips,),
            in_specs=[
                pl.BlockSpec((2 * m, depth), lambda i, s: (s[0] ^ i, 0)),
                whole((depth, t)),
                whole((depth, t)),
            ],
            out_specs=(block, block),
            scratch_shapes=[pltpu.VMEM((depth, 2 * t), bf16), pltpu.VMEM((PAD, t), f32)],
        ),
        out_shape=(out, out),
        compiler_params=params(),
        cost_estimate=cost(8 * n * depth * t, 4 * n * depth),
    )(place, inv_factor, direction, residual)


def kernel_kernel(segments, place, own_ref, other_ref, c_ref, high_ref, low_ref, ph, plo, psq):
    @pl.when(pl.program_id(0) == 0)
    def _():
        n = own_ref.shape[0]
        seg = n // segments
        for side, ref in enumerate((own_ref, other_ref)):
            for u in range(segments):
                start = pl.multiple_of((place[2] ^ u) * seg, seg)
                p = ref[pl.ds(start, seg), :]
                at = slice(side * n + u * seg, side * n + (u + 1) * seg)
                ph[at, :], plo[at, :] = split(p)
                psq[at, :] = jnp.broadcast_to(0.5 * jnp.sum(p * p, axis=1, keepdims=True), (seg, 128))

    c = c_ref[...]
    ch, cl = split(c)
    x = lax.dot_general(ch, ph[...], LAST, preferred_element_type=f32)
    x += lax.dot_general(ch, plo[...], LAST, preferred_element_type=f32)
    x += lax.dot_general(cl, ph[...], LAST, preferred_element_type=f32)
    center_sq = 0.5 * jnp.sum(c * c, axis=1, keepdims=True)
    point_sq = psq[...].T[0:1, :]
    high_ref[0], low_ref[0] = split(jnp.exp(x - (center_sq + point_sq)))


def gaussian(place, own, other, centers, chips, segments):
    n, width = own.shape
    m = centers.shape[0] // chips // 2
    out = jax.ShapeDtypeStruct((chips, m, 2 * n), bf16)
    block = pl.BlockSpec((1, m, 2 * n), lambda i, s: (i, 0, 0))
    return pl.pallas_call(
        functools.partial(kernel_kernel, segments),
        grid_spec=pltpu.PrefetchScalarGridSpec(
            num_scalar_prefetch=1,
            grid=(chips,),
            in_specs=[
                whole((n, width)),
                whole((n, width)),
                pl.BlockSpec((m, width), lambda i, s: (2 * (s[0] ^ i) + s[1], 0)),
            ],
            out_specs=(block, block),
            scratch_shapes=[
                pltpu.VMEM((2 * n, width), bf16),
                pltpu.VMEM((2 * n, width), bf16),
                pltpu.VMEM((2 * n, 128), f32),
            ],
        ),
        out_shape=(out, out),
        compiler_params=params(),
        cost_estimate=cost(12 * chips * m * n * width, 8 * chips * m * n, 2 * chips * m * n),
    )(place, own, other, centers)


def predict_kernel(first, n_pieces, last, *refs):
    high_ref, low_ref = refs[:2]
    pieces = refs[2 : 2 + n_pieces]
    rest = refs[2 + n_pieces :]
    if first:
        acc = rest[0]
    else:
        start_ref, keep_ref, send_ref, acc = rest
    i = pl.program_id(0)
    m = high_ref.shape[1]
    for j, piece in enumerate(pieces):

        @pl.when(i == j)
        def _(j=j, piece=piece):
            value = turned(pair(piece[:m, :]), high_ref[0], low_ref[0])
            if first and j == 0:
                acc[...] = value
            elif j == 0:
                acc[...] = start_ref[...] + value
            else:
                acc[...] += value

    if last:

        @pl.when(i == n_pieces - 1)
        def _():
            half = keep_ref.shape[0]
            keep_ref[...] = acc[:, :half].T
            send_ref[...] = acc[:, half:].T


def predict(high, low, pieces, offset, start=None):
    _, m, n = high.shape
    t = pieces[0].shape[1]
    first = start is None
    k_block = pl.BlockSpec((1, m, n), lambda i: (i + offset, 0, 0))
    in_specs = [k_block, k_block] + [whole(p.shape) for p in pieces]
    args = [high, low, *pieces]
    if first:
        out_shape, out_specs = jax.ShapeDtypeStruct((t, n), f32), whole((t, n))
        scratch = []
    else:
        in_specs.append(whole((t, n)))
        args.append(start)
        out_shape = (jax.ShapeDtypeStruct((n // 2, t), f32),) * 2
        out_specs = (whole((n // 2, t)),) * 2
        scratch = [pltpu.VMEM((t, n), f32)]
    return pl.pallas_call(
        functools.partial(predict_kernel, first, len(pieces), not first),
        grid=(len(pieces),),
        in_specs=in_specs,
        out_specs=out_specs,
        out_shape=out_shape,
        scratch_shapes=scratch,
        compiler_params=params(),
        cost_estimate=cost(8 * len(pieces) * m * n * t, 4 * len(pieces) * m * n),
    )(*args)


def back_kernel(high_ref, low_ref, own_ref, other_ref, out_ref, pairs, norms):
    half = own_ref.shape[0]

    @pl.when(pl.program_id(0) == 0)
    def _():
        norms[...] = jnp.zeros_like(norms)
        a, b = own_ref[...], other_ref[...]
        pairs[:half, :] = pair(a)
        pairs[half:, :] = pair(b)
        norms[0:1, :] = jnp.sum(a * a, axis=0, keepdims=True) + jnp.sum(b * b, axis=0, keepdims=True)

    m = high_ref.shape[1]
    n = out_ref.shape[2]
    both = jnp.dot(high_ref[0], pairs[...], preferred_element_type=f32)
    both += jnp.dot(low_ref[0], pairs[...], preferred_element_type=f32)
    out_ref[0, :m, :] = both[:, :n] + both[:, n:]
    out_ref[0, m:, :] = norms[...]


def back_product(high, low, own, other):
    chips, m, n = high.shape
    t = own.shape[1]
    k_block = pl.BlockSpec((1, m, n), lambda i: (i, 0, 0))
    return pl.pallas_call(
        back_kernel,
        grid=(chips,),
        in_specs=[k_block, k_block, whole(own.shape), whole(other.shape)],
        out_specs=pl.BlockSpec((1, m + PAD, t), lambda i: (i, 0, 0)),
        out_shape=jax.ShapeDtypeStruct((chips, m + PAD, t), f32),
        scratch_shapes=[pltpu.VMEM((n, 2 * t), bf16), pltpu.VMEM((PAD, t), f32)],
        compiler_params=params(),
        cost_estimate=cost(8 * chips * m * n * t, 4 * chips * m * n),
    )(high, low, own, other)


def transposed_kernel(first, n_pieces, segments, place, l_ref, *refs):
    own, other = refs[:n_pieces], refs[n_pieces : 2 * n_pieces]
    rest = refs[2 * n_pieces :]
    if first:
        acc, pairs = rest
    else:
        start_ref, keep_ref, send_ref, acc, pairs, image = rest
    i = pl.program_id(0)
    m = l_ref.shape[0] // 2
    core = place[1]
    for j in range(n_pieces):

        @pl.when(i == j)
        def _(j=j):
            pairs[pl.ds(pl.multiple_of(core * m, m), m), :] = pair(own[j][:m, :])
            pairs[pl.ds(pl.multiple_of((1 - core) * m, m), m), :] = pair(other[j][:m, :])

    high, low = split(l_ref[...])
    value = turned(pairs[...], high, low)

    @pl.when(i == 0)
    def _():
        acc[...] = value if first else start_ref[...] + value

    @pl.when(i > 0)
    def _():
        acc[...] += value

    if not first:

        @pl.when(i == n_pieces - 1)
        def _():
            image[...] = acc[...].T
            seg = image.shape[0] // segments
            half = segments // 2
            for u in range(segments):
                ref = keep_ref if u < half else send_ref
                at = pl.ds(pl.multiple_of((place[2] ^ u) * seg, seg), seg)
                ref[(u % half) * seg : (u % half + 1) * seg, :] = image[at, :]


def transposed(place, inv_factor, own, other, offset, chips, segments, start=None):
    n, depth = inv_factor.shape
    m = n // chips // 2
    t = own[0].shape[1]
    first = start is None
    pieces = len(own)
    in_specs = [pl.BlockSpec((2 * m, depth), lambda i, s: (s[0] ^ (i + offset), 0))]
    in_specs += [whole(p.shape) for p in (*own, *other)]
    args = [inv_factor, *own, *other]
    scratch = [pltpu.VMEM((2 * m, 2 * t), bf16)]
    if first:
        out_shape, out_specs = jax.ShapeDtypeStruct((t, depth), f32), whole((t, depth))
    else:
        in_specs.append(whole((t, depth)))
        args.append(start)
        out_shape = (jax.ShapeDtypeStruct((depth // 2, t), f32),) * 2
        out_specs = (whole((depth // 2, t)),) * 2
        scratch = [pltpu.VMEM((t, depth), f32), *scratch, pltpu.VMEM((depth, t), f32)]
    return pl.pallas_call(
        functools.partial(transposed_kernel, first, pieces, segments),
        grid_spec=pltpu.PrefetchScalarGridSpec(
            num_scalar_prefetch=1,
            grid=(pieces,),
            in_specs=in_specs,
            out_specs=out_specs,
            scratch_shapes=scratch,
        ),
        out_shape=out_shape,
        compiler_params=params(),
        cost_estimate=cost(16 * pieces * m * depth * t, 8 * pieces * m * depth),
    )(place, *args)


def update_kernel(place, image_ref, r_ref, d_ref, own_ref, norm_ref, new_ref, sum_ref):
    m = own_ref.shape[0] - PAD
    norm_now, dir_norm = norm_ref[0:1, :], norm_ref[1:2, :]
    curvature = own_ref[m : m + 1, :] + ridge_weight * dir_norm
    step = norm_now / curvature
    new = r_ref[...] - step * (image_ref[...] + ridge_weight * d_ref[...])
    new_ref[...] = new
    sum_ref[...] = jnp.broadcast_to(jnp.sum(new * new, axis=0, keepdims=True), sum_ref.shape)


def update(place, image, residual, direction, back_own, norms, segments):
    seg, t = image.shape
    at = pl.BlockSpec((seg, t), lambda i, s: (s[2], 0))
    return pl.pallas_call(
        update_kernel,
        grid_spec=pltpu.PrefetchScalarGridSpec(
            num_scalar_prefetch=1,
            grid=(1,),
            in_specs=[whole((seg, t)), at, at, whole(back_own.shape), whole(norms.shape)],
            out_specs=(whole((seg, t)), whole((PAD, t))),
        ),
        out_shape=(jax.ShapeDtypeStruct((seg, t), f32), jax.ShapeDtypeStruct((PAD, t), f32)),
        compiler_params=params(),
    )(place, image, residual, direction, back_own, norms)


def finish_kernel(n_pieces, place, *refs):
    pieces = refs[:n_pieces]
    d_ref, norm_ref, next_ref, res_ref, dir_ref = refs[n_pieces:]
    ratio = next_ref[0:1, :] / norm_ref[0:1, :]
    seg = pieces[0].shape[0]
    u = 0
    for piece in pieces:
        for j in range(piece.shape[0] // seg):
            at = pl.ds(pl.multiple_of((place[2] ^ u) * seg, seg), seg)
            new = piece[j * seg : (j + 1) * seg, :]
            res_ref[at, :] = new
            dir_ref[at, :] = new + ratio * d_ref[at, :]
            u += 1


def finish(place, pieces, direction, norms, norm_next):
    out = jax.ShapeDtypeStruct(direction.shape, f32)
    args = [*pieces, direction, norms, norm_next]
    return pl.pallas_call(
        functools.partial(finish_kernel, len(pieces)),
        grid_spec=pltpu.PrefetchScalarGridSpec(
            num_scalar_prefetch=1,
            grid=(1,),
            in_specs=[whole(a.shape) for a in args],
            out_specs=(whole(direction.shape),) * 2,
        ),
        out_shape=(out, out),
        compiler_params=params(),
    )(place, *args)


def body(n_rows, n_cols, points, centers, inv_factor, solution, residual, direction):
    chips = n_rows // 2
    steps = n_cols.bit_length() - 1
    masks = [(2 << s) - 1 for s in range(steps)]

    def swap(x, axis, mask):
        size = n_rows if axis == "rows" else n_cols
        return lax.ppermute(x, axis, [(i, i ^ mask) for i in range(size)])

    row, col = lax.axis_index("rows"), lax.axis_index("cols")
    segment = 0
    for s in range(steps):
        bit = (col >> s) & 1
        if s + 1 < steps:
            bit = bit ^ ((col >> (s + 1)) & 1)
        segment = segment | (bit << (steps - 1 - s))
    place = jnp.stack([row // 2, row % 2, segment]).astype(jnp.int32)

    order = [chips - 1, *range(1, chips - 1)] if chips > 1 else []

    def scatter(parts):
        got = [swap(parts[i], "rows", 2 * i) for i in order]
        return sum(got, parts[0])

    def gather(own):
        got = {i: swap(own, "rows", 2 * i) for i in order}
        return [got[i] for i in range(1, chips)]

    other_points = swap(points, "rows", 1)
    keep, send = forward(place, inv_factor, direction, residual, chips)
    got = swap(send, "rows", 1)
    mapped = scatter([keep[i] + got[i] for i in range(chips)])
    m = mapped.shape[0] - PAD
    norms = mapped[m:]
    high, low = gaussian(place, points, other_points, centers, chips, n_cols)
    mapped_own = mapped[:m]
    first = predict(high, low, [mapped_own], 0)
    keep, send = predict(high, low, gather(mapped_own), 1, first)
    part = keep + swap(send, "rows", 1)
    for mask in masks:
        half = part.shape[0] // 2
        part = part[:half] + swap(part[half:], "cols", mask)
    for mask in masks[::-1]:
        part = jnp.concatenate([part, swap(part, "cols", mask)], axis=0)
    other = swap(part, "rows", 1)
    backs = back_product(high, low, part, other)
    back = scatter([backs[i] for i in range(chips)])
    back_own = back[:m]
    first = transposed(place, inv_factor, [back_own], [swap(back_own, "rows", 1)], 0, chips, n_cols)
    got = gather(back_own)
    keep, send = transposed(
        place, inv_factor, got, [swap(g, "rows", 1) for g in got], 1, chips, n_cols, first
    )
    image = keep + swap(send, "cols", masks[0])
    for mask in masks[1:]:
        half = image.shape[0] // 2
        image = image[:half] + swap(image[half:], "cols", mask)
    new_piece, norm_next = update(place, image, residual, direction, back, norms, n_cols)
    mask = 1
    while mask < n_rows:
        norm_next = norm_next + swap(norm_next, "rows", mask)
        mask *= 2
    pieces = [new_piece]
    gathered = new_piece
    for mask in masks[::-1]:
        got = swap(gathered, "cols", mask)
        pieces.append(got)
        gathered = jnp.concatenate([gathered, got], axis=0)
        norm_next = norm_next + swap(norm_next, "cols", mask)
    step = norms[0:1] / (back[m : m + 1] + ridge_weight * norms[1:2])
    new_solution = solution + step * direction
    new_residual, new_direction = finish(place, pieces, direction, norms, norm_next)
    return new_solution, new_residual, new_direction


def solution(mesh):
    return jax.shard_map(
        functools.partial(body, mesh.shape["rows"], mesh.shape["cols"]),
        mesh=mesh,
        in_specs=(
            P("rows", None),
            P("cols", None),
            P("cols", "rows"),
            P("rows", None),
            P("rows", None),
            P("rows", None),
        ),
        out_specs=(P("rows", None), P("rows", None), P("rows", None)),
        check_vma=False,
    )
```

```python
import functools

import jax
import jax.numpy as jnp
from jax import lax
from jax.experimental import pallas as pl
from jax.experimental.pallas import tpu as pltpu
from jax.sharding import PartitionSpec as P

ridge_weight = 0.02
PAD = 8
f32, bf16 = jnp.float32, jnp.bfloat16
FIRST = (((0,), (0,)), ((), ()))
LAST = (((1,), (1,)), ((), ()))


def split(value):
    high = value.astype(bf16)
    return high, (value - high.astype(f32)).astype(bf16)


def pair(value):
    high, low = split(value)
    return jnp.concatenate([high, low], axis=1)


def wide(lhs, pairs, dims=None):
    high, low = split(lhs)
    n = pairs.shape[1] // 2
    both = jnp.dot(high, pairs, preferred_element_type=f32)
    both += jnp.dot(low, pairs, preferred_element_type=f32)
    return both[:, :n] + both[:, n:]


def turned(pairs, high, low):
    n = pairs.shape[1] // 2
    both = lax.dot_general(pairs, high, FIRST, preferred_element_type=f32)
    both += lax.dot_general(pairs, low, FIRST, preferred_element_type=f32)
    return both[:n] + both[n:]


def params(mib=10):
    return pltpu.CompilerParams(vmem_limit_bytes=mib << 20)


def cost(*_):
    return pl.CostEstimate(flops=1, bytes_accessed=1, transcendentals=0)


local = pl.BlockSpec(memory_space=pltpu.VMEM)
scalars = pl.BlockSpec(memory_space=pltpu.SMEM)


def whole(shape):
    return pl.BlockSpec(shape, lambda *_: (0,) * len(shape))


def resident(x):
    return pltpu.with_memory_space_constraint(x, pltpu.VMEM)


def forward_kernel(place, l_ref, d_ref, r_ref, keep_ref, send_ref, pairs, norms):
    @pl.when(pl.program_id(0) == 0)
    def _():
        d, r = d_ref[...], r_ref[...]
        pairs[...] = pair(d)
        norms[...] = jnp.zeros_like(norms)
        norms[0:1, :] = jnp.sum(r * r, axis=0, keepdims=True)
        norms[1:2, :] = jnp.sum(d * d, axis=0, keepdims=True)

    m = l_ref.shape[0] // 2
    core = place[1]
    for out_ref, side in ((keep_ref, core), (send_ref, 1 - core)):
        rows = l_ref[pl.ds(pl.multiple_of(side * m, m), m), :]
        out_ref[0, :m, :] = wide(rows, pairs[...])
        out_ref[0, m:, :] = norms[...]


def forward(place, inv_factor, direction, residual, chips):
    n, depth = inv_factor.shape
    t = direction.shape[1]
    m = n // chips // 2
    out = jax.ShapeDtypeStruct((chips, m + PAD, t), f32)
    block = pl.BlockSpec((1, m + PAD, t), lambda i, s: (i, 0, 0))
    return pl.pallas_call(
        forward_kernel,
        grid_spec=pltpu.PrefetchScalarGridSpec(
            num_scalar_prefetch=1,
            grid=(chips,),
            in_specs=[
                pl.BlockSpec((2 * m, depth), lambda i, s: (s[0] ^ i, 0)),
                whole((depth, t)),
                whole((depth, t)),
            ],
            out_specs=(block, block),
            scratch_shapes=[pltpu.VMEM((depth, 2 * t), bf16), pltpu.VMEM((PAD, t), f32)],
        ),
        out_shape=(out, out),
        compiler_params=params(40),
        cost_estimate=cost(8 * n * depth * t, 4 * n * depth),
    )(place, inv_factor, direction, residual)


def add_kernel(n_terms, *refs):
    terms, outs = refs[:n_terms], refs[n_terms:]
    if len(outs) > 1 and len(terms[0].shape) == 3:
        for i, out in enumerate(outs):
            out[...] = terms[0][i] + terms[1][i]
        return
    value = terms[0][...]
    for term in terms[1:]:
        value += term[...]
    start = 0
    for out in outs:
        out[...] = value[start : start + out.shape[0], :]
        start += out.shape[0]


def add(terms, shapes):
    out = tuple(jax.ShapeDtypeStruct(shape, f32) for shape in shapes)
    return pl.pallas_call(
        functools.partial(add_kernel, len(terms)),
        in_specs=[local] * len(terms),
        out_specs=(local,) * len(out),
        out_shape=out,
        compiler_params=params(),
        cost_estimate=cost(),
    )(*terms)


def kernel_kernel(segments, place, own_ref, other_ref, c_ref, high_ref, low_ref, ph, plo, psq):
    @pl.when(pl.program_id(0) == 0)
    def _():
        n = own_ref.shape[0]
        seg = n // segments
        for side, ref in enumerate((own_ref, other_ref)):
            for u in range(segments):
                start = pl.multiple_of((place[2] ^ u) * seg, seg)
                p = ref[pl.ds(start, seg), :]
                at = slice(side * n + u * seg, side * n + (u + 1) * seg)
                ph[at, :], plo[at, :] = split(p)
                psq[at, :] = jnp.broadcast_to(0.5 * jnp.sum(p * p, axis=1, keepdims=True), (seg, 128))

    c = c_ref[...]
    ch, cl = split(c)
    x = lax.dot_general(ch, ph[...], LAST, preferred_element_type=f32)
    x += lax.dot_general(ch, plo[...], LAST, preferred_element_type=f32)
    x += lax.dot_general(cl, ph[...], LAST, preferred_element_type=f32)
    center_sq = 0.5 * jnp.sum(c * c, axis=1, keepdims=True)
    point_sq = psq[...].T[0:1, :]
    high_ref[0], low_ref[0] = split(jnp.exp(x - (center_sq + point_sq)))


def gaussian(place, own, other, centers, chips, segments):
    n, width = own.shape
    m = centers.shape[0] // chips // 2
    out = jax.ShapeDtypeStruct((chips, m, 2 * n), bf16)
    block = pl.BlockSpec((1, m, 2 * n), lambda i, s: (i, 0, 0))
    return pl.pallas_call(
        functools.partial(kernel_kernel, segments),
        grid_spec=pltpu.PrefetchScalarGridSpec(
            num_scalar_prefetch=1,
            grid=(chips,),
            in_specs=[
                whole((n, width)),
                whole((n, width)),
                pl.BlockSpec((m, width), lambda i, s: (2 * (s[0] ^ i) + s[1], 0)),
            ],
            out_specs=(block, block),
            scratch_shapes=[
                pltpu.VMEM((2 * n, width), bf16),
                pltpu.VMEM((2 * n, width), bf16),
                pltpu.VMEM((2 * n, 128), f32),
            ],
        ),
        out_shape=(out, out),
        compiler_params=params(),
        cost_estimate=cost(12 * chips * m * n * width, 8 * chips * m * n, 2 * chips * m * n),
    )(place, own, other, centers)


def predict_kernel(shift, first, last, high_ref, low_ref, piece_ref, *refs):
    m = high_ref.shape[1]
    value = turned(pair(piece_ref[:m, :]), high_ref[shift], low_ref[shift])
    if not first:
        value += refs[0][...]
    if last:
        half = value.shape[1] // 2
        refs[-2][...] = value[:, :half].T
        refs[-1][...] = value[:, half:].T
    else:
        refs[-1][...] = value


def predict(shift, high, low, piece, acc, last):
    _, m, n = high.shape
    t = piece.shape[1]
    args = [resident(high), resident(low), piece] + ([] if acc is None else [acc])
    if last:
        out = (jax.ShapeDtypeStruct((n // 2, t), f32),) * 2
    else:
        out = jax.ShapeDtypeStruct((t, n), f32)
    return pl.pallas_call(
        functools.partial(predict_kernel, shift, acc is None, last),
        in_specs=[local] * len(args),
        out_specs=(local,) * 2 if last else local,
        out_shape=out,
        compiler_params=params(),
        cost_estimate=cost(8 * m * n * t, 4 * m * n),
    )(*args)


def back_kernel(shift, first, high_ref, low_ref, *refs):
    if first:
        own_ref, other_ref, out_ref, pairs, norms = refs
        half = own_ref.shape[0]
        norms[...] = jnp.zeros_like(norms)
        a, b = own_ref[...], other_ref[...]
        pairs[:half, :] = pair(a)
        pairs[half:, :] = pair(b)
        norms[0:1, :] = jnp.sum(a * a, axis=0, keepdims=True) + jnp.sum(b * b, axis=0, keepdims=True)
    else:
        pairs, norms, out_ref = refs
    m = high_ref.shape[1]
    n = out_ref.shape[1]
    both = jnp.dot(high_ref[shift], pairs[...], preferred_element_type=f32)
    both += jnp.dot(low_ref[shift], pairs[...], preferred_element_type=f32)
    out_ref[:m, :] = both[:, :n] + both[:, n:]
    out_ref[m:, :] = norms[...]


def back_product(shift, high, low, sources, first):
    _, m, n = high.shape
    t = sources[1].shape[1]
    out = (jax.ShapeDtypeStruct((m + PAD, t), f32),)
    if first:
        out += (jax.ShapeDtypeStruct((n, 2 * t), bf16), jax.ShapeDtypeStruct((PAD, t), f32))
    return pl.pallas_call(
        functools.partial(back_kernel, shift, first),
        in_specs=[local] * 4,
        out_specs=(local,) * len(out),
        out_shape=out,
        compiler_params=params(),
        cost_estimate=cost(8 * m * n * t, 4 * m * n),
    )(resident(high), resident(low), *sources)


def transposed_kernel(shift, sides, first, segments, place, l_ref, *refs):
    pieces, refs = refs[: len(sides)], refs[len(sides) :]
    value = None if first else refs[0][...]
    block = place[0] ^ shift
    for side, ref in zip(sides, pieces):
        core = place[1] if side == 0 else 1 - place[1]
        m = ref.shape[0]
        step = min(m, 256)
        for i in range(0, m, step):
            start = pl.multiple_of((block * 2 + core) * m + i, step)
            high, low = split(l_ref[pl.ds(start, step), :])
            share = turned(pair(ref[i : i + step, :]), high, low)
            value = share if value is None else value + share
    if segments == 0:
        refs[-1][...] = value
        return
    keep_ref, send_ref, image = refs[-3:]
    image[...] = value.T
    seg = image.shape[0] // segments
    half = segments // 2
    for u in range(segments):
        ref = keep_ref if u < half else send_ref
        at = pl.ds(pl.multiple_of((place[2] ^ u) * seg, seg), seg)
        ref[(u % half) * seg : (u % half + 1) * seg, :] = image[at, :]


def transposed(shift, sides, place, inv_factor, pieces, acc, segments=0):
    depth = inv_factor.shape[1]
    m, t = pieces[0].shape
    args = [resident(inv_factor), *pieces] + ([] if acc is None else [acc])
    scratch = []
    if segments:
        out = (jax.ShapeDtypeStruct((depth // 2, t), f32),) * 2
        scratch = [pltpu.VMEM((depth, t), f32)]
    else:
        out = jax.ShapeDtypeStruct((t, depth), f32)
    return pl.pallas_call(
        functools.partial(transposed_kernel, shift, sides, acc is None, segments),
        in_specs=[scalars] + [local] * len(args),
        out_specs=(local,) * 2 if segments else local,
        out_shape=out,
        scratch_shapes=scratch,
        compiler_params=params(),
        cost_estimate=cost(),
    )(place, *args)


def update_kernel(place, image_ref, r_ref, d_ref, pred_ref, norm_ref, new_ref, sum_ref):
    norm_now, dir_norm = norm_ref[0:1, :], norm_ref[1:2, :]
    curvature = pred_ref[0:1, :] + ridge_weight * dir_norm
    step = norm_now / curvature
    new = r_ref[...] - step * (image_ref[...] + ridge_weight * d_ref[...])
    new_ref[...] = new
    sum_ref[...] = jnp.broadcast_to(jnp.sum(new * new, axis=0, keepdims=True), sum_ref.shape)


def update(place, image, residual, direction, pred_norm, norms, segments):
    seg, t = image.shape
    at = pl.BlockSpec((seg, t), lambda i, s: (s[2], 0))
    return pl.pallas_call(
        update_kernel,
        grid_spec=pltpu.PrefetchScalarGridSpec(
            num_scalar_prefetch=1,
            grid=(1,),
            in_specs=[whole((seg, t)), at, at, whole(pred_norm.shape), whole(norms.shape)],
            out_specs=(whole((seg, t)), whole((PAD, t))),
        ),
        out_shape=(jax.ShapeDtypeStruct((seg, t), f32), jax.ShapeDtypeStruct((PAD, t), f32)),
        compiler_params=params(),
    )(place, image, residual, direction, pred_norm, norms)


def finish_kernel(n_pieces, place, *refs):
    pieces = refs[:n_pieces]
    d_ref, norm_ref, next_ref, res_ref, dir_ref = refs[n_pieces:]
    ratio = next_ref[0:1, :] / norm_ref[0:1, :]
    seg = pieces[0].shape[0]
    u = 0
    for piece in pieces:
        for j in range(piece.shape[0] // seg):
            at = pl.ds(pl.multiple_of((place[2] ^ u) * seg, seg), seg)
            new = piece[j * seg : (j + 1) * seg, :]
            res_ref[at, :] = new
            dir_ref[at, :] = new + ratio * d_ref[at, :]
            u += 1


def finish(place, pieces, direction, norms, norm_next):
    out = jax.ShapeDtypeStruct(direction.shape, f32)
    args = [*pieces, direction, norms, norm_next]
    return pl.pallas_call(
        functools.partial(finish_kernel, len(pieces)),
        grid_spec=pltpu.PrefetchScalarGridSpec(
            num_scalar_prefetch=1,
            grid=(1,),
            in_specs=[whole(a.shape) for a in args],
            out_specs=(whole(direction.shape),) * 2,
        ),
        out_shape=(out, out),
        compiler_params=params(),
    )(place, *args)


def body(n_rows, n_cols, points, centers, inv_factor, solution, residual, direction):
    chips = n_rows // 2
    steps = n_cols.bit_length() - 1
    masks = [(2 << s) - 1 for s in range(steps)]
    halving, last_mask = masks[:-1], masks[-1]
    segments = n_cols // 2

    def swap(x, axis, mask):
        size = n_rows if axis == "rows" else n_cols
        return lax.ppermute(x, axis, [(i, i ^ mask) for i in range(size)])

    row, col = lax.axis_index("rows"), lax.axis_index("cols")
    segment = 0
    for s in range(steps - 1):
        bit = ((col >> s) ^ (col >> (s + 1))) & 1
        segment = segment | (bit << (steps - 2 - s))
    place = jnp.stack([row // 2, row % 2, segment]).astype(jnp.int32)
    order = [chips - 1, *range(1, chips - 1)]

    other_points = swap(points, "rows", 1)
    keep, send = forward(place, inv_factor, direction, residual, chips)
    m, t = keep.shape[1] - PAD, keep.shape[2]
    totals = add([keep, swap(send, "rows", 1)], [(m + PAD, t)] * chips)
    got = [swap(totals[i], "rows", 2 * i) for i in order]
    mapped, norms = add([totals[0], *got], [(m, t), (PAD, t)])
    high, low = gaussian(place, points, other_points, centers, chips, segments)
    mapped, high, low = lax.optimization_barrier((mapped, high, low))

    arrived = [(0, mapped)] + [(i, swap(mapped, "rows", 2 * i)) for i in order]
    acc = None
    for j, (shift, piece) in enumerate(arrived):
        acc = predict(shift, high, low, piece, acc, j == chips - 1)
    keep, send = acc
    part = keep + swap(send, "rows", 1)
    for mask in halving:
        half = part.shape[0] // 2
        part = part[:half] + swap(part[half:], "cols", mask)
    part = part + swap(part, "cols", last_mask)
    for mask in halving[::-1]:
        part = jnp.concatenate([part, swap(part, "cols", mask)], axis=0)
    other = swap(part, "rows", 1)

    got = []
    sources, first = (part, other), True
    for shift in (*order, 0):
        piece, *rest = back_product(shift, high, low, sources, first)
        if first:
            sources, first = rest, False
        got.append(swap(piece, "rows", 2 * shift) if shift else piece)
    own, pred_norm = add([got[-1], *got[:-1]], [(m, t), (PAD, t)])

    arrived = [(i, swap(own, "rows", 2 * i)) for i in order]
    acc = transposed(0, (0, 1), place, inv_factor, [own, swap(own, "rows", 1)], None)
    others = []
    for shift, piece in arrived:
        piece, acc = lax.optimization_barrier((piece, acc))
        others.append((shift, swap(piece, "rows", 1)))
        acc = transposed(shift, (0,), place, inv_factor, [piece], acc)
    for j, (shift, piece) in enumerate(others):
        last = j == chips - 2
        acc = transposed(shift, (1,), place, inv_factor, [piece], acc, segments if last else 0)
    keep, send = acc
    image = keep + swap(send, "cols", masks[0])
    for mask in halving[1:]:
        half = image.shape[0] // 2
        image = image[:half] + swap(image[half:], "cols", mask)
    image = image + swap(image, "cols", last_mask)
    new_piece, norm_next = update(place, image, residual, direction, pred_norm, norms, segments)
    pieces = [new_piece]
    gathered = new_piece
    for mask in halving[::-1]:
        got = swap(gathered, "cols", mask)
        pieces.append(got)
        gathered = jnp.concatenate([gathered, got], axis=0)
    for mask in halving[::-1]:
        norm_next = norm_next + swap(norm_next, "cols", mask)
    norm_next = jnp.sum(lax.all_gather(norm_next, "rows"), axis=0)
    step = norms[0:1] / (pred_norm[0:1] + ridge_weight * norms[1:2])
    new_solution = solution + step * direction
    new_residual, new_direction = finish(place, pieces, direction, norms, norm_next)
    return new_solution, new_residual, new_direction


def solution(mesh):
    return jax.shard_map(
        functools.partial(body, mesh.shape["rows"], mesh.shape["cols"]),
        mesh=mesh,
        in_specs=(
            P("rows", None),
            P("cols", None),
            P("cols", "rows"),
            P("rows", None),
            P("rows", None),
            P("rows", None),
        ),
        out_specs=(P("rows", None), P("rows", None), P("rows", None)),
        check_vma=False,
    )
```

```python
import functools

import jax
import jax.numpy as jnp
from jax import lax
from jax.experimental import pallas as pl
from jax.experimental.pallas import tpu as pltpu
from jax.sharding import PartitionSpec as P

ridge_weight = 0.02
PAD = 8
SHARES = (1, 3)
f32, bf16 = jnp.float32, jnp.bfloat16
FIRST = (((0,), (0,)), ((), ()))
LAST = (((1,), (1,)), ((), ()))


def split(value):
    high = value.astype(bf16)
    return high, (value - high.astype(f32)).astype(bf16)


def pair(value):
    high, low = split(value)
    return jnp.concatenate([high, low], axis=1)


def wide(lhs, pairs, dims=None):
    high, low = split(lhs)
    n = pairs.shape[1] // 2
    both = jnp.dot(high, pairs, preferred_element_type=f32)
    both += jnp.dot(low, pairs, preferred_element_type=f32)
    return both[:, :n] + both[:, n:]


def turned(pairs, high, low):
    n = pairs.shape[1] // 2
    both = lax.dot_general(pairs, high, FIRST, preferred_element_type=f32)
    both += lax.dot_general(pairs, low, FIRST, preferred_element_type=f32)
    return both[:n] + both[n:]


def params(mib=10):
    return pltpu.CompilerParams(vmem_limit_bytes=mib << 20)


def cost(*_):
    return pl.CostEstimate(flops=1, bytes_accessed=1, transcendentals=0)


local = pl.BlockSpec(memory_space=pltpu.VMEM)
scalars = pl.BlockSpec(memory_space=pltpu.SMEM)


def whole(shape):
    return pl.BlockSpec(shape, lambda *_: (0,) * len(shape))


def here(n_cols):
    row, col = lax.axis_index("rows"), lax.axis_index("cols")
    steps = n_cols.bit_length() - 1
    segment = 0
    for s in range(steps - 1):
        bit = ((col >> s) ^ (col >> (s + 1))) & 1
        segment = segment | (bit << (steps - 2 - s))
    return row >> 1, row & 1, segment


def cuts(rows):
    ends = [rows * sum(SHARES[: i + 1]) // sum(SHARES) for i in range(len(SHARES))]
    return list(zip([0, *ends], ends))


def resident(x):
    return pltpu.with_memory_space_constraint(x, pltpu.VMEM)


def forward_kernel(chips, slots, l_ref, d_ref, r_ref, keep_ref, send_ref, buffer, arrived, d, r, pairs, sems):
    m = buffer.shape[1]
    jobs = 2 * chips
    chip, core, _ = here(2)

    def copy(t, side):
        n = 2 * t + side
        start = pl.multiple_of(((chip ^ t) * 2 + (core ^ side)) * m, m)
        slot = lax.rem(n, slots)
        return pltpu.make_async_copy(l_ref.at[pl.ds(start, m), :], buffer.at[slot], arrived.at[slot])

    copy_d = pltpu.make_async_copy(d_ref, d, sems.at[0])
    copy_r = pltpu.make_async_copy(r_ref, r, sems.at[1])
    copy_d.start()
    for n in range(min(slots - 1, jobs)):
        copy(n // 2, n % 2).start()
    copy_r.start()
    copy_d.wait()
    pairs[...] = pair(d[...])

    def step(n, carry):
        ahead = n + slots - 1

        @pl.when(ahead < jobs)
        def _():
            copy(ahead >> 1, ahead & 1).start()

        copy(n >> 1, n & 1).wait()
        value = wide(buffer[lax.rem(n, slots)], pairs[...])

        @pl.when(n & 1 == 0)
        def _():
            keep_ref[n >> 1, :m, :] = value

        @pl.when(n & 1 == 1)
        def _():
            send_ref[n >> 1, :m, :] = value

        return carry

    lax.fori_loop(0, jobs, step, 0)
    copy_r.wait()
    norm_now = jnp.sum(r[...] * r[...], axis=0, keepdims=True)
    dir_norm = jnp.sum(d[...] * d[...], axis=0, keepdims=True)
    for ref in (keep_ref, send_ref):
        for t in range(chips):
            ref[t, m:, :] = jnp.zeros((PAD, d.shape[1]), f32)
            ref[t, m : m + 1, :] = norm_now
            ref[t, m + 1 : m + 2, :] = dir_norm


def forward(inv_factor, direction, residual, chips):
    n, depth = inv_factor.shape
    t = direction.shape[1]
    m = n // chips // 2
    out = jax.ShapeDtypeStruct((chips, m + PAD, t), f32)
    slots = 3
    far = pl.BlockSpec(memory_space=pl.ANY)
    return pl.pallas_call(
        functools.partial(forward_kernel, chips, slots),
        in_specs=[far] * 3,
        out_specs=(local, local),
        out_shape=(out, out),
        scratch_shapes=[
            pltpu.VMEM((slots, m, depth), f32),
            pltpu.SemaphoreType.DMA((slots,)),
            pltpu.VMEM((depth, t), f32),
            pltpu.VMEM((depth, t), f32),
            pltpu.VMEM((depth, 2 * t), bf16),
            pltpu.SemaphoreType.DMA((2,)),
        ],
        compiler_params=params(40),
        cost_estimate=cost(),
    )(*[pltpu.with_memory_space_constraint(x, pltpu.HBM) for x in (inv_factor, direction, residual)])


def add_kernel(n_terms, n_held, *refs):
    terms, outs = refs[:n_terms], refs[n_terms + n_held :]
    if len(outs) > 1 and len(terms[0].shape) == 3:
        for i, out in enumerate(outs):
            out[...] = terms[0][i] + terms[1][i]
        return
    value = terms[0][...]
    for term in terms[1:]:
        value += term[...]
    start = 0
    for out in outs:
        out[...] = value[start : start + out.shape[0], :]
        start += out.shape[0]


def add(terms, shapes, held=()):
    out = tuple(jax.ShapeDtypeStruct(shape, f32) for shape in shapes)
    return pl.pallas_call(
        functools.partial(add_kernel, len(terms), len(held)),
        in_specs=[local] * (len(terms) + len(held)),
        out_specs=(local,) * len(out),
        out_shape=out,
        compiler_params=params(),
        cost_estimate=cost(),
    )(*terms, *map(resident, held))


def kernel_kernel(segments, place, own_ref, other_ref, c_ref, high_ref, low_ref, ph, plo, psq):
    @pl.when(pl.program_id(0) == 0)
    def _():
        n = own_ref.shape[0]
        seg = n // segments
        for side, ref in enumerate((own_ref, other_ref)):
            for u in range(segments):
                start = pl.multiple_of((place[2] ^ u) * seg, seg)
                p = ref[pl.ds(start, seg), :]
                at = slice(side * n + u * seg, side * n + (u + 1) * seg)
                ph[at, :], plo[at, :] = split(p)
                psq[at, :] = jnp.broadcast_to(0.5 * jnp.sum(p * p, axis=1, keepdims=True), (seg, 128))

    c = c_ref[...]
    ch, cl = split(c)
    x = lax.dot_general(ch, ph[...], LAST, preferred_element_type=f32)
    x += lax.dot_general(ch, plo[...], LAST, preferred_element_type=f32)
    x += lax.dot_general(cl, ph[...], LAST, preferred_element_type=f32)
    center_sq = 0.5 * jnp.sum(c * c, axis=1, keepdims=True)
    point_sq = psq[...].T[0:1, :]
    high_ref[0], low_ref[0] = split(jnp.exp(x - (center_sq + point_sq)))


def gaussian(place, own, other, centers, chips, segments):
    n, width = own.shape
    m = centers.shape[0] // chips // 2
    out = jax.ShapeDtypeStruct((chips, m, 2 * n), bf16)
    block = pl.BlockSpec((1, m, 2 * n), lambda i, s: (i, 0, 0))
    return pl.pallas_call(
        functools.partial(kernel_kernel, segments),
        grid_spec=pltpu.PrefetchScalarGridSpec(
            num_scalar_prefetch=1,
            grid=(chips,),
            in_specs=[
                whole((n, width)),
                whole((n, width)),
                pl.BlockSpec((m, width), lambda i, s: (2 * (s[0] ^ i) + s[1], 0)),
            ],
            out_specs=(block, block),
            scratch_shapes=[
                pltpu.VMEM((2 * n, width), bf16),
                pltpu.VMEM((2 * n, width), bf16),
                pltpu.VMEM((2 * n, 128), f32),
            ],
        ),
        out_shape=(out, out),
        compiler_params=params(),
        cost_estimate=cost(12 * chips * m * n * width, 8 * chips * m * n, 2 * chips * m * n),
    )(place, own, other, centers)


def predict_kernel(shift, first, last, high_ref, low_ref, piece_ref, *refs):
    m = high_ref.shape[1]
    value = turned(pair(piece_ref[:m, :]), high_ref[shift], low_ref[shift])
    if not first:
        value += refs[0][...]
    if last:
        half = value.shape[1] // 2
        refs[-2][...] = value[:, :half].T
        refs[-1][...] = value[:, half:].T
    else:
        refs[-1][...] = value


def predict(shift, high, low, piece, acc, last):
    _, m, n = high.shape
    t = piece.shape[1]
    args = [resident(high), resident(low), piece] + ([] if acc is None else [acc])
    if last:
        out = (jax.ShapeDtypeStruct((n // 2, t), f32),) * 2
    else:
        out = jax.ShapeDtypeStruct((t, n), f32)
    return pl.pallas_call(
        functools.partial(predict_kernel, shift, acc is None, last),
        in_specs=[local] * len(args),
        out_specs=(local,) * 2 if last else local,
        out_shape=out,
        compiler_params=params(),
        cost_estimate=cost(8 * m * n * t, 4 * m * n),
    )(*args)


def back_kernel(shift, first, high_ref, low_ref, *refs):
    refs = refs[1:] if shift == 0 else refs
    if first:
        own_ref, other_ref, out_ref, pairs, norms = refs
        half = own_ref.shape[0]
        norms[...] = jnp.zeros_like(norms)
        a, b = own_ref[...], other_ref[...]
        pairs[:half, :] = pair(a)
        pairs[half:, :] = pair(b)
        norms[0:1, :] = jnp.sum(a * a, axis=0, keepdims=True) + jnp.sum(b * b, axis=0, keepdims=True)
    else:
        pairs, norms, out_ref = refs
    m = high_ref.shape[1]
    n = out_ref.shape[1]
    both = jnp.dot(high_ref[shift], pairs[...], preferred_element_type=f32)
    both += jnp.dot(low_ref[shift], pairs[...], preferred_element_type=f32)
    out_ref[:m, :] = both[:, :n] + both[:, n:]
    out_ref[m:, :] = norms[...]


def back_product(shift, high, low, sources, first, held=()):
    _, m, n = high.shape
    t = sources[1].shape[1]
    out = (jax.ShapeDtypeStruct((m + PAD, t), f32),)
    if first:
        out += (jax.ShapeDtypeStruct((n, 2 * t), bf16), jax.ShapeDtypeStruct((PAD, t), f32))
    return pl.pallas_call(
        functools.partial(back_kernel, shift, first),
        in_specs=[local] * (4 + len(held)),
        out_specs=(local,) * len(out),
        out_shape=out,
        compiler_params=params(),
        cost_estimate=cost(8 * m * n * t, 4 * m * n),
    )(resident(high), resident(low), *map(resident, held), *sources)


def transposed_kernel(shift, sides, first, segments, l_ref, *refs):
    place = here(2 * segments)
    pieces, refs = refs[: len(sides)], refs[len(sides) :]
    value = None if first else refs[0][...]
    block = place[0] ^ shift
    for side, ref in zip(sides, pieces):
        core = place[1] if side == 0 else 1 - place[1]
        m = ref.shape[0]
        step = min(m, 256)
        for i in range(0, m, step):
            start = pl.multiple_of((block * 2 + core) * m + i, step)
            high, low = split(l_ref[pl.ds(start, step), :])
            share = turned(pair(ref[i : i + step, :]), high, low)
            value = share if value is None else value + share
    if segments == 0:
        refs[-1][...] = value
        return
    *outs, image = refs[-2 * len(SHARES) - 1 :]
    image[...] = value.T
    seg = image.shape[0] // segments
    half = segments // 2
    for u in range(segments):
        for c, (begin, end) in enumerate(cuts(seg)):
            ref = outs[2 * c + (u >= half)]
            at = pl.ds(pl.multiple_of((place[2] ^ u) * seg + begin, PAD), end - begin)
            start = (u % half) * (end - begin)
            ref[start : start + end - begin, :] = image[at, :]


def transposed(shift, sides, inv_factor, pieces, acc, segments=0):
    depth = inv_factor.shape[1]
    m, t = pieces[0].shape
    args = [resident(inv_factor), *pieces] + ([] if acc is None else [acc])
    scratch = []
    if segments:
        seg = depth // segments
        out = tuple(
            jax.ShapeDtypeStruct((segments // 2 * (end - begin), t), f32)
            for begin, end in cuts(seg)
            for _ in range(2)
        )
        scratch = [pltpu.VMEM((depth, t), f32)]
    else:
        out = jax.ShapeDtypeStruct((t, depth), f32)
    return pl.pallas_call(
        functools.partial(transposed_kernel, shift, sides, acc is None, segments),
        in_specs=[local] * len(args),
        out_specs=(local,) * len(out) if segments else local,
        out_shape=out,
        scratch_shapes=scratch,
        compiler_params=params(),
        cost_estimate=cost(),
    )(*args)


def update_kernel(begin, rows, segments, image_ref, r_ref, d_ref, pred_ref, norm_ref, *refs):
    new_ref, sum_ref = refs[-2:]
    norm_now, dir_norm = norm_ref[0:1, :], norm_ref[1:2, :]
    curvature = pred_ref[0:1, :] + ridge_weight * dir_norm
    step = norm_now / curvature
    start = here(2 * segments)[2] * rows + begin
    at = pl.ds(pl.multiple_of(start, PAD), image_ref.shape[0])
    new = r_ref[at, :] - step * (image_ref[...] + ridge_weight * d_ref[at, :])
    new_ref[...] = new
    total = jnp.broadcast_to(jnp.sum(new * new, axis=0, keepdims=True), sum_ref.shape)
    if len(refs) == 3:
        total += refs[0][...]
    sum_ref[...] = total


def update(begin, image, residual, direction, pred_norm, norms, before, segments):
    rows = residual.shape[0] // segments
    args = [image, residual, direction, pred_norm, norms] + ([] if before is None else [before])
    out = (jax.ShapeDtypeStruct(image.shape, f32), jax.ShapeDtypeStruct(norms.shape, f32))
    return pl.pallas_call(
        functools.partial(update_kernel, begin, rows, segments),
        in_specs=[local] * len(args),
        out_specs=(local, local),
        out_shape=out,
        compiler_params=params(),
        cost_estimate=cost(),
    )(*args)


def finish_kernel(segments, n_pieces, *refs):
    pieces = refs[:n_pieces]
    d_ref, norm_ref, next_ref, res_ref, dir_ref = refs[n_pieces:]
    ratio = next_ref[0:1, :] / norm_ref[0:1, :]
    segment = here(2 * segments)[2]
    seg = d_ref.shape[0] // segments
    each = n_pieces // len(SHARES)
    for c, (begin, end) in enumerate(cuts(seg)):
        n = end - begin
        u = 0
        for piece in pieces[c * each : (c + 1) * each]:
            for j in range(piece.shape[0] // n):
                at = pl.ds(pl.multiple_of((segment ^ u) * seg + begin, PAD), n)
                new = piece[j * n : (j + 1) * n, :]
                res_ref[at, :] = new
                dir_ref[at, :] = new + ratio * d_ref[at, :]
                u += 1


def finish(pieces, direction, norms, norm_next, segments):
    out = jax.ShapeDtypeStruct(direction.shape, f32)
    args = [*pieces, direction, norms, norm_next]
    return pl.pallas_call(
        functools.partial(finish_kernel, segments, len(pieces)),
        in_specs=[local] * len(args),
        out_specs=(local, local),
        out_shape=(out, out),
        compiler_params=params(),
        cost_estimate=cost(),
    )(*args)


def body(n_rows, n_cols, points, centers, inv_factor, solution, residual, direction):
    chips = n_rows // 2
    steps = n_cols.bit_length() - 1
    masks = [(2 << s) - 1 for s in range(steps)]
    halving, last_mask = masks[:-1], masks[-1]
    segments = n_cols // 2

    def swap(x, axis, mask):
        size = n_rows if axis == "rows" else n_cols
        return lax.ppermute(x, axis, [(i, i ^ mask) for i in range(size)])

    place = jnp.stack(here(n_cols)).astype(jnp.int32)
    order = [chips - 1, *range(1, chips - 1)]

    other_points = swap(points, "rows", 1)
    keep, send = forward(inv_factor, direction, residual, chips)
    m, t = keep.shape[1] - PAD, keep.shape[2]
    totals = add([keep, swap(send, "rows", 1)], [(m + PAD, t)] * chips)
    got = [swap(totals[i], "rows", 2 * i) for i in order]
    mapped, norms = add([totals[0], *got], [(m, t), (PAD, t)])
    high, low = gaussian(place, points, other_points, centers, chips, segments)
    mapped, high, low = lax.optimization_barrier((mapped, high, low))

    arrived = [(0, mapped)] + [(i, swap(mapped, "rows", 2 * i)) for i in order]
    acc = None
    for j, (shift, piece) in enumerate(arrived):
        acc = predict(shift, high, low, piece, acc, j == chips - 1)
    keep, send = acc
    part = keep + swap(send, "rows", 1)
    for mask in halving:
        half = part.shape[0] // 2
        part = part[:half] + swap(part[half:], "cols", mask)
    part = part + swap(part, "cols", last_mask)
    for mask in halving[::-1]:
        part = jnp.concatenate([part, swap(part, "cols", mask)], axis=0)
    other = swap(part, "rows", 1)

    got = []
    sources, first = (part, other), True
    for shift in (*order, 0):
        piece, *rest = back_product(
            shift, high, low, sources, first, () if shift else (inv_factor,)
        )
        if first:
            sources, first = rest, False
        got.append(swap(piece, "rows", 2 * shift) if shift else piece)
    own, pred_norm = add([got[-1], *got[:-1]], [(m, t), (PAD, t)], (inv_factor,))

    arrived = [(i, swap(own, "rows", 2 * i)) for i in order]
    acc = transposed(0, (0, 1), inv_factor, [own, swap(own, "rows", 1)], None)
    late = []
    for shift, piece in arrived:
        piece, acc = lax.optimization_barrier((piece, acc))
        other = swap(piece, "rows", 1)
        acc = transposed(shift, (0,), inv_factor, [piece], acc)
        late.append((shift, other))
    for shift, other in late:
        last = shift == late[-1][0]
        acc = transposed(shift, (1,), inv_factor, [other], acc, segments if last else 0)
    pieces, norm_next, step_one, step_two, done = [], None, (), (), ()
    for c, (begin, _) in enumerate(cuts(residual.shape[0] // segments)):
        image, send = acc[2 * c : 2 * c + 2]
        send, step_one = lax.optimization_barrier((send, step_one))
        step_one = swap(send, "cols", masks[0])
        image = image + step_one
        for mask in halving[1:]:
            half = image.shape[0] // 2
            image = image[:half] + swap(image[half:], "cols", mask)
        image, step_two = lax.optimization_barrier((image, step_two))
        step_two = swap(image, "cols", last_mask)
        image = image + step_two
        image, done = lax.optimization_barrier((image, done))
        new, norm_next = update(
            begin, image, residual, direction, pred_norm, norms, norm_next, segments
        )
        pieces.append(new)
        for mask in halving[::-1]:
            done = swap(new, "cols", mask)
            pieces.append(done)
            new = jnp.concatenate([new, done], axis=0)
    for mask in halving[::-1]:
        norm_next = norm_next + swap(norm_next, "cols", mask)
    norm_next = jnp.sum(lax.all_gather(norm_next, "rows"), axis=0)
    step = norms[0:1] / (pred_norm[0:1] + ridge_weight * norms[1:2])
    new_solution = solution + step * direction
    new_residual, new_direction = finish(
        pieces, direction, norms, norm_next, segments
    )
    return new_solution, new_residual, new_direction


def solution(mesh):
    return jax.shard_map(
        functools.partial(body, mesh.shape["rows"], mesh.shape["cols"]),
        mesh=mesh,
        in_specs=(
            P("rows", None),
            P("cols", None),
            P("cols", "rows"),
            P("rows", None),
            P("rows", None),
            P("rows", None),
        ),
        out_specs=(P("rows", None), P("rows", None), P("rows", None)),
        check_vma=False,
    )
```

```python
import functools

import jax
import jax.numpy as jnp
from jax import lax
from jax.experimental import pallas as pl
from jax.experimental.pallas import tpu as pltpu
from jax.sharding import PartitionSpec as P

ridge_weight = 0.02
PAD = 8
SHARES = (1, 3)
f32, bf16 = jnp.float32, jnp.bfloat16
FIRST = (((0,), (0,)), ((), ()))
LAST = (((1,), (1,)), ((), ()))


def split(value):
    high = value.astype(bf16)
    return high, (value - high.astype(f32)).astype(bf16)


def pair(value):
    high, low = split(value)
    return jnp.concatenate([high, low], axis=1)


def wide(lhs, pairs, dims=None):
    high, low = split(lhs)
    n = pairs.shape[1] // 2
    both = jnp.dot(high, pairs, preferred_element_type=f32)
    both += jnp.dot(low, pairs, preferred_element_type=f32)
    return both[:, :n] + both[:, n:]


def turned(pairs, high, low):
    n = pairs.shape[1] // 2
    both = lax.dot_general(pairs, high, FIRST, preferred_element_type=f32)
    both += lax.dot_general(pairs, low, FIRST, preferred_element_type=f32)
    return both[:n] + both[n:]


def params(mib=10):
    return pltpu.CompilerParams(vmem_limit_bytes=mib << 20)


def cost(*_):
    return pl.CostEstimate(flops=1, bytes_accessed=1, transcendentals=0)


local = pl.BlockSpec(memory_space=pltpu.VMEM)
scalars = pl.BlockSpec(memory_space=pltpu.SMEM)


def whole(shape):
    return pl.BlockSpec(shape, lambda *_: (0,) * len(shape))


def here(n_cols):
    row, col = lax.axis_index("rows"), lax.axis_index("cols")
    steps = n_cols.bit_length() - 1
    segment = 0
    for s in range(steps - 1):
        bit = ((col >> s) ^ (col >> (s + 1))) & 1
        segment = segment | (bit << (steps - 2 - s))
    return row >> 1, row & 1, segment


def cuts(rows):
    ends = [rows * sum(SHARES[: i + 1]) // sum(SHARES) for i in range(len(SHARES))]
    return list(zip([0, *ends], ends))


def resident(x):
    return pltpu.with_memory_space_constraint(x, pltpu.VMEM)


def forward_kernel(chips, slots, l_ref, d_ref, r_ref, keep_ref, send_ref, buffer, arrived, d, r, pairs, sems):
    m = buffer.shape[1]
    jobs = 2 * chips
    chip, core, _ = here(2)

    def copy(t, side):
        n = 2 * t + side
        start = pl.multiple_of(((chip ^ t) * 2 + (core ^ side)) * m, m)
        slot = lax.rem(n, slots)
        return pltpu.make_async_copy(l_ref.at[pl.ds(start, m), :], buffer.at[slot], arrived.at[slot])

    copy_d = pltpu.make_async_copy(d_ref, d, sems.at[0])
    copy_r = pltpu.make_async_copy(r_ref, r, sems.at[1])
    copy_d.start()
    for n in range(min(slots - 1, jobs)):
        copy(n // 2, n % 2).start()
    copy_r.start()
    copy_d.wait()
    pairs[...] = pair(d[...])

    def step(n, carry):
        ahead = n + slots - 1

        @pl.when(ahead < jobs)
        def _():
            copy(ahead >> 1, ahead & 1).start()

        copy(n >> 1, n & 1).wait()
        value = wide(buffer[lax.rem(n, slots)], pairs[...])

        @pl.when(n & 1 == 0)
        def _():
            keep_ref[n >> 1, :m, :] = value

        @pl.when(n & 1 == 1)
        def _():
            send_ref[n >> 1, :m, :] = value

        return carry

    lax.fori_loop(0, jobs, step, 0)
    copy_r.wait()
    norm_now = jnp.sum(r[...] * r[...], axis=0, keepdims=True)
    dir_norm = jnp.sum(d[...] * d[...], axis=0, keepdims=True)
    for ref in (keep_ref, send_ref):
        for t in range(chips):
            ref[t, m:, :] = jnp.zeros((PAD, d.shape[1]), f32)
            ref[t, m : m + 1, :] = norm_now
            ref[t, m + 1 : m + 2, :] = dir_norm


def forward(inv_factor, direction, residual, chips):
    n, depth = inv_factor.shape
    t = direction.shape[1]
    m = n // chips // 2
    out = jax.ShapeDtypeStruct((chips, m + PAD, t), f32)
    slots = 3
    far = pl.BlockSpec(memory_space=pl.ANY)
    return pl.pallas_call(
        functools.partial(forward_kernel, chips, slots),
        in_specs=[far] * 3,
        out_specs=(local, local),
        out_shape=(out, out),
        scratch_shapes=[
            pltpu.VMEM((slots, m, depth), f32),
            pltpu.SemaphoreType.DMA((slots,)),
            pltpu.VMEM((depth, t), f32),
            pltpu.VMEM((depth, t), f32),
            pltpu.VMEM((depth, 2 * t), bf16),
            pltpu.SemaphoreType.DMA((2,)),
        ],
        compiler_params=params(40),
        cost_estimate=cost(),
    )(*[pltpu.with_memory_space_constraint(x, pltpu.HBM) for x in (inv_factor, direction, residual)])


def add_kernel(n_terms, n_held, *refs):
    terms, outs = refs[:n_terms], refs[n_terms + n_held :]
    if len(outs) > 1 and len(terms[0].shape) == 3:
        for i, out in enumerate(outs):
            out[...] = terms[0][i] + terms[1][i]
        return
    value = terms[0][...]
    for term in terms[1:]:
        value += term[...]
    start = 0
    for out in outs:
        out[...] = value[start : start + out.shape[0], :]
        start += out.shape[0]


def add(terms, shapes, held=()):
    out = tuple(jax.ShapeDtypeStruct(shape, f32) for shape in shapes)
    return pl.pallas_call(
        functools.partial(add_kernel, len(terms), len(held)),
        in_specs=[local] * (len(terms) + len(held)),
        out_specs=(local,) * len(out),
        out_shape=out,
        compiler_params=params(),
        cost_estimate=cost(),
    )(*terms, *map(resident, held))


def kernel_kernel(segments, place, own_ref, other_ref, c_ref, high_ref, low_ref, ph, plo, psq):
    @pl.when(pl.program_id(0) == 0)
    def _():
        n = own_ref.shape[0]
        seg = n // segments
        for side, ref in enumerate((own_ref, other_ref)):
            for u in range(segments):
                start = pl.multiple_of((place[2] ^ u) * seg, seg)
                p = ref[pl.ds(start, seg), :]
                at = slice(side * n + u * seg, side * n + (u + 1) * seg)
                ph[at, :], plo[at, :] = split(p)
                psq[at, :] = jnp.broadcast_to(0.5 * jnp.sum(p * p, axis=1, keepdims=True), (seg, 128))

    c = c_ref[...]
    ch, cl = split(c)
    x = lax.dot_general(ch, ph[...], LAST, preferred_element_type=f32)
    x += lax.dot_general(ch, plo[...], LAST, preferred_element_type=f32)
    x += lax.dot_general(cl, ph[...], LAST, preferred_element_type=f32)
    center_sq = 0.5 * jnp.sum(c * c, axis=1, keepdims=True)
    point_sq = psq[...].T[0:1, :]
    high_ref[0], low_ref[0] = split(jnp.exp(x - (center_sq + point_sq)))


def gaussian(place, own, other, centers, chips, segments):
    n, width = own.shape
    m = centers.shape[0] // chips // 2
    out = jax.ShapeDtypeStruct((chips, m, 2 * n), bf16)
    block = pl.BlockSpec((1, m, 2 * n), lambda i, s: (i, 0, 0))
    return pl.pallas_call(
        functools.partial(kernel_kernel, segments),
        grid_spec=pltpu.PrefetchScalarGridSpec(
            num_scalar_prefetch=1,
            grid=(chips,),
            in_specs=[
                whole((n, width)),
                whole((n, width)),
                pl.BlockSpec((m, width), lambda i, s: (2 * (s[0] ^ i) + s[1], 0)),
            ],
            out_specs=(block, block),
            scratch_shapes=[
                pltpu.VMEM((2 * n, width), bf16),
                pltpu.VMEM((2 * n, width), bf16),
                pltpu.VMEM((2 * n, 128), f32),
            ],
        ),
        out_shape=(out, out),
        compiler_params=params(),
        cost_estimate=cost(12 * chips * m * n * width, 8 * chips * m * n, 2 * chips * m * n),
    )(place, own, other, centers)


def predict_kernel(shift, first, last, high_ref, low_ref, piece_ref, *refs):
    m = high_ref.shape[1]
    value = turned(pair(piece_ref[:m, :]), high_ref[shift], low_ref[shift])
    if not first:
        value += refs[0][...]
    if last:
        half = value.shape[1] // 2
        refs[-2][...] = value[:, :half].T
        refs[-1][...] = value[:, half:].T
    else:
        refs[-1][...] = value


def predict(shift, high, low, piece, acc, last):
    _, m, n = high.shape
    t = piece.shape[1]
    args = [resident(high), resident(low), piece] + ([] if acc is None else [acc])
    if last:
        out = (jax.ShapeDtypeStruct((n // 2, t), f32),) * 2
    else:
        out = jax.ShapeDtypeStruct((t, n), f32)
    return pl.pallas_call(
        functools.partial(predict_kernel, shift, acc is None, last),
        in_specs=[local] * len(args),
        out_specs=(local,) * 2 if last else local,
        out_shape=out,
        compiler_params=params(),
        cost_estimate=cost(8 * m * n * t, 4 * m * n),
    )(*args)


def back_kernel(shift, first, high_ref, low_ref, *refs):
    refs = refs[1:] if shift == 0 else refs
    if first:
        own_ref, other_ref, out_ref, pairs, norms = refs
        half = own_ref.shape[0]
        norms[...] = jnp.zeros_like(norms)
        a, b = own_ref[...], other_ref[...]
        pairs[:half, :] = pair(a)
        pairs[half:, :] = pair(b)
        norms[0:1, :] = jnp.sum(a * a, axis=0, keepdims=True) + jnp.sum(b * b, axis=0, keepdims=True)
    else:
        pairs, norms, out_ref = refs
    m = high_ref.shape[1]
    n = out_ref.shape[1]
    both = jnp.dot(high_ref[shift], pairs[...], preferred_element_type=f32)
    both += jnp.dot(low_ref[shift], pairs[...], preferred_element_type=f32)
    out_ref[:m, :] = both[:, :n] + both[:, n:]
    out_ref[m:, :] = norms[...]


def back_product(shift, high, low, sources, first, held=()):
    _, m, n = high.shape
    t = sources[1].shape[1]
    out = (jax.ShapeDtypeStruct((m + PAD, t), f32),)
    if first:
        out += (jax.ShapeDtypeStruct((n, 2 * t), bf16), jax.ShapeDtypeStruct((PAD, t), f32))
    return pl.pallas_call(
        functools.partial(back_kernel, shift, first),
        in_specs=[local] * (4 + len(held)),
        out_specs=(local,) * len(out),
        out_shape=out,
        compiler_params=params(),
        cost_estimate=cost(8 * m * n * t, 4 * m * n),
    )(resident(high), resident(low), *map(resident, held), *sources)


def transposed_kernel(shift, sides, first, l_ref, *refs):
    place = here(2)
    pieces, refs = refs[: len(sides)], refs[len(sides) :]
    value = None if first else refs[0][...]
    block = place[0] ^ shift
    for side, ref in zip(sides, pieces):
        core = place[1] if side == 0 else 1 - place[1]
        m = ref.shape[0]
        step = min(m, 256)
        for i in range(0, m, step):
            start = pl.multiple_of((block * 2 + core) * m + i, step)
            high, low = split(l_ref[pl.ds(start, step), :])
            share = turned(pair(ref[i : i + step, :]), high, low)
            value = share if value is None else value + share
    refs[-1][...] = value


def transposed(shift, sides, inv_factor, pieces, acc):
    depth = inv_factor.shape[1]
    t = pieces[0].shape[1]
    args = [resident(inv_factor), *pieces] + ([] if acc is None else [acc])
    return pl.pallas_call(
        functools.partial(transposed_kernel, shift, sides, acc is None),
        in_specs=[local] * len(args),
        out_specs=local,
        out_shape=jax.ShapeDtypeStruct((t, depth), f32),
        compiler_params=params(),
        cost_estimate=cost(),
    )(*args)


def last_kernel(shifts, part, segments, l_ref, acc_ref, *refs):
    pieces, (keep_ref, send_ref, image) = refs[: len(shifts)], refs[len(shifts) :]
    chip, core, segment = here(2 * segments)
    m, depth = pieces[0].shape[0], acc_ref.shape[1]
    seg, n = depth // segments, image.shape[1]
    begin, end = cuts(seg)[part]
    bands = [(u * seg + begin, u * seg + end) for u in range(segments)]
    apart = all(edge % 128 == 0 for band in bands for edge in band)
    pairs = [pair(ref[...]) for ref in pieces]
    for u, (low_edge, high_edge) in enumerate(bands if apart else [(0, depth)]):
        value = acc_ref[:, low_edge:high_edge]
        for shift, values in zip(shifts, pairs):
            start = pl.multiple_of(((chip ^ shift) * 2 + 1 - core) * m, m)
            high, low = split(l_ref[pl.ds(start, m), low_edge:high_edge])
            value += turned(values, high, low)
        value = value.T
        if apart:
            image[u] = value
        else:
            for i, (first, final) in enumerate(bands):
                image[i] = value[first:final, :]
    half = segments // 2
    for u in range(segments):
        ref = keep_ref if u < half else send_ref
        ref[(u % half) * n : (u % half + 1) * n, :] = image[segment ^ u]


def last_transposed(part, segments, inv_factor, pieces, acc):
    t, depth = acc.shape
    begin, end = cuts(depth // segments)[part]
    out = jax.ShapeDtypeStruct((segments // 2 * (end - begin), t), f32)
    args = [resident(inv_factor), acc, *[piece for _, piece in pieces]]
    return pl.pallas_call(
        functools.partial(last_kernel, [shift for shift, _ in pieces], part, segments),
        in_specs=[local] * len(args),
        out_specs=(local, local),
        out_shape=(out, out),
        scratch_shapes=[pltpu.VMEM((segments, end - begin, t), f32)],
        compiler_params=params(),
        cost_estimate=cost(),
    )(*args)


def update_kernel(begin, rows, segments, image_ref, r_ref, d_ref, pred_ref, norm_ref, *refs):
    new_ref, sum_ref = refs[-2:]
    norm_now, dir_norm = norm_ref[0:1, :], norm_ref[1:2, :]
    curvature = pred_ref[0:1, :] + ridge_weight * dir_norm
    step = norm_now / curvature
    start = here(2 * segments)[2] * rows + begin
    at = pl.ds(pl.multiple_of(start, PAD), image_ref.shape[0])
    new = r_ref[at, :] - step * (image_ref[...] + ridge_weight * d_ref[at, :])
    new_ref[...] = new
    total = jnp.broadcast_to(jnp.sum(new * new, axis=0, keepdims=True), sum_ref.shape)
    if len(refs) == 3:
        total += refs[0][...]
    sum_ref[...] = total


def update(begin, image, residual, direction, pred_norm, norms, before, segments):
    rows = residual.shape[0] // segments
    args = [image, residual, direction, pred_norm, norms] + ([] if before is None else [before])
    out = (jax.ShapeDtypeStruct(image.shape, f32), jax.ShapeDtypeStruct(norms.shape, f32))
    return pl.pallas_call(
        functools.partial(update_kernel, begin, rows, segments),
        in_specs=[local] * len(args),
        out_specs=(local, local),
        out_shape=out,
        compiler_params=params(),
        cost_estimate=cost(),
    )(*args)


def finish_kernel(segments, n_pieces, *refs):
    pieces = refs[:n_pieces]
    d_ref, norm_ref, next_ref, res_ref, dir_ref = refs[n_pieces:]
    ratio = next_ref[0:1, :] / norm_ref[0:1, :]
    segment = here(2 * segments)[2]
    seg = d_ref.shape[0] // segments
    each = n_pieces // len(SHARES)
    for c, (begin, end) in enumerate(cuts(seg)):
        n = end - begin
        u = 0
        for piece in pieces[c * each : (c + 1) * each]:
            for j in range(piece.shape[0] // n):
                at = pl.ds(pl.multiple_of((segment ^ u) * seg + begin, PAD), n)
                new = piece[j * n : (j + 1) * n, :]
                res_ref[at, :] = new
                dir_ref[at, :] = new + ratio * d_ref[at, :]
                u += 1


def finish(pieces, direction, norms, norm_next, segments):
    out = jax.ShapeDtypeStruct(direction.shape, f32)
    args = [*pieces, direction, norms, norm_next]
    return pl.pallas_call(
        functools.partial(finish_kernel, segments, len(pieces)),
        in_specs=[local] * len(args),
        out_specs=(local, local),
        out_shape=(out, out),
        compiler_params=params(),
        cost_estimate=cost(),
    )(*args)


def body(n_rows, n_cols, points, centers, inv_factor, solution, residual, direction):
    chips = n_rows // 2
    steps = n_cols.bit_length() - 1
    masks = [(2 << s) - 1 for s in range(steps)]
    halving, last_mask = masks[:-1], masks[-1]
    segments = n_cols // 2

    def swap(x, axis, mask):
        size = n_rows if axis == "rows" else n_cols
        return lax.ppermute(x, axis, [(i, i ^ mask) for i in range(size)])

    place = jnp.stack(here(n_cols)).astype(jnp.int32)
    order = list(range(1, chips))

    other_points = swap(points, "rows", 1)
    keep, send = forward(inv_factor, direction, residual, chips)
    m, t = keep.shape[1] - PAD, keep.shape[2]
    totals = add([keep, swap(send, "rows", 1)], [(m + PAD, t)] * chips)
    got = [swap(totals[i], "rows", 2 * i) for i in order]
    mapped, norms = add([totals[0], *got], [(m, t), (PAD, t)])
    high, low = gaussian(place, points, other_points, centers, chips, segments)
    mapped, high, low = lax.optimization_barrier((mapped, high, low))

    arrived = [(0, mapped)] + [(i, swap(mapped, "rows", 2 * i)) for i in order]
    acc = None
    for j, (shift, piece) in enumerate(arrived):
        acc = predict(shift, high, low, piece, acc, j == chips - 1)
    keep, send = acc
    part = keep + swap(send, "rows", 1)
    for mask in halving:
        half = part.shape[0] // 2
        part = part[:half] + swap(part[half:], "cols", mask)
    part = part + swap(part, "cols", last_mask)
    for mask in halving[::-1]:
        part = jnp.concatenate([part, swap(part, "cols", mask)], axis=0)
    other = swap(part, "rows", 1)

    got = []
    sources, first = (part, other), True
    for shift in (*order, 0):
        piece, *rest = back_product(
            shift, high, low, sources, first, () if shift else (inv_factor,)
        )
        if first:
            sources, first = rest, False
        got.append(swap(piece, "rows", 2 * shift) if shift else piece)
    own, pred_norm = add([got[-1], *got[:-1]], [(m, t), (PAD, t)], (inv_factor,))

    arrived = [(i, swap(own, "rows", 2 * i)) for i in order]
    acc = transposed(0, (0, 1), inv_factor, [own, swap(own, "rows", 1)], None)
    late = []
    for shift, piece in arrived:
        piece, acc = lax.optimization_barrier((piece, acc))
        other = swap(piece, "rows", 1)
        acc = transposed(shift, (0,), inv_factor, [piece], acc)
        late.append((shift, other))
    pieces, norm_next, step_one, step_two, done = [], None, (), (), ()
    for c, (begin, _) in enumerate(cuts(residual.shape[0] // segments)):
        image, send = last_transposed(c, segments, inv_factor, late, acc)
        send, step_one = lax.optimization_barrier((send, step_one))
        step_one = swap(send, "cols", masks[0])
        image = image + step_one
        for mask in halving[1:]:
            half = image.shape[0] // 2
            image = image[:half] + swap(image[half:], "cols", mask)
        image, step_two = lax.optimization_barrier((image, step_two))
        step_two = swap(image, "cols", last_mask)
        image = image + step_two
        image, done = lax.optimization_barrier((image, done))
        new, norm_next = update(
            begin, image, residual, direction, pred_norm, norms, norm_next, segments
        )
        pieces.append(new)
        for mask in halving[::-1]:
            done = swap(new, "cols", mask)
            pieces.append(done)
            new = jnp.concatenate([new, done], axis=0)
    for mask in halving[::-1]:
        norm_next = norm_next + swap(norm_next, "cols", mask)
    norm_next = jnp.sum(lax.all_gather(norm_next, "rows"), axis=0)
    step = norms[0:1] / (pred_norm[0:1] + ridge_weight * norms[1:2])
    new_solution = solution + step * direction
    new_residual, new_direction = finish(
        pieces, direction, norms, norm_next, segments
    )
    return new_solution, new_residual, new_direction


def solution(mesh):
    return jax.shard_map(
        functools.partial(body, mesh.shape["rows"], mesh.shape["cols"]),
        mesh=mesh,
        in_specs=(
            P("rows", None),
            P("cols", None),
            P("cols", "rows"),
            P("rows", None),
            P("rows", None),
            P("rows", None),
        ),
        out_specs=(P("rows", None), P("rows", None), P("rows", None)),
        check_vma=False,
    )
```

```python
import functools

import jax
import jax.numpy as jnp
from jax import lax
from jax.experimental import pallas as pl
from jax.experimental.pallas import tpu as pltpu
from jax.sharding import PartitionSpec as P

ridge_weight = 0.02
PAD = 8
SHARES = (1, 3)
f32, bf16 = jnp.float32, jnp.bfloat16
FIRST = (((0,), (0,)), ((), ()))
LAST = (((1,), (1,)), ((), ()))


def split(value):
    high = value.astype(bf16)
    return high, (value - high.astype(f32)).astype(bf16)


def pair(value):
    high, low = split(value)
    return jnp.concatenate([high, low], axis=1)


def wide(lhs, pairs, dims=None):
    high, low = split(lhs)
    n = pairs.shape[1] // 2
    both = jnp.dot(high, pairs, preferred_element_type=f32)
    both += jnp.dot(low, pairs, preferred_element_type=f32)
    return both[:, :n] + both[:, n:]


def turned(pairs, high, low):
    n = pairs.shape[1] // 2
    both = lax.dot_general(pairs, high, FIRST, preferred_element_type=f32)
    both += lax.dot_general(pairs, low, FIRST, preferred_element_type=f32)
    return both[:n] + both[n:]


def params(mib=10):
    return pltpu.CompilerParams(vmem_limit_bytes=mib << 20)


def cost(*_):
    return pl.CostEstimate(flops=1, bytes_accessed=1, transcendentals=0)


local = pl.BlockSpec(memory_space=pltpu.VMEM)
scalars = pl.BlockSpec(memory_space=pltpu.SMEM)


def whole(shape):
    return pl.BlockSpec(shape, lambda *_: (0,) * len(shape))


def here(n_cols):
    row, col = lax.axis_index("rows"), lax.axis_index("cols")
    steps = n_cols.bit_length() - 1
    segment = 0
    for s in range(steps - 1):
        bit = ((col >> s) ^ (col >> (s + 1))) & 1
        segment = segment | (bit << (steps - 2 - s))
    return row >> 1, row & 1, segment


def cuts(rows):
    ends = [rows * sum(SHARES[: i + 1]) // sum(SHARES) for i in range(len(SHARES))]
    return list(zip([0, *ends], ends))


def resident(x):
    return pltpu.with_memory_space_constraint(x, pltpu.VMEM)


def forward_kernel(chips, begin, end, slots, l_ref, d_ref, r_ref, *refs):
    *outs, buffer, arrived, d, r, pairs, sems = refs
    m = buffer.shape[1]
    chip, core, _ = here(2)
    kept = chips - outs[0].shape[0] if begin == 0 else 0

    def job(n):
        return chips - 1 - (n >> 1), 1 - (n & 1)

    def copy(n):
        t, side = job(n)
        start = pl.multiple_of(((chip ^ t) * 2 + (core ^ side)) * m, m)
        slot = lax.rem(n, slots)
        return pltpu.make_async_copy(l_ref.at[pl.ds(start, m), :], buffer.at[slot], arrived.at[slot])

    copy_d = pltpu.make_async_copy(d_ref, d, sems.at[0])
    copy_r = pltpu.make_async_copy(r_ref, r, sems.at[1])
    copy_d.start()
    for n in range(begin, min(begin + slots - 1, end)):
        copy(n).start()
    copy_r.start()
    copy_d.wait()
    pairs[...] = pair(d[...])

    def step(n, carry):
        @pl.when(n + slots - 1 < end)
        def _():
            copy(n + slots - 1).start()

        copy(n).wait()
        value = wide(buffer[lax.rem(n, slots)], pairs[...])
        t, side = job(n)
        if begin:
            outs[0][t, :m, :] = value
            return carry

        @pl.when(side == 0)
        def _():
            outs[0][t - kept, :m, :] = value

        @pl.when(side == 1)
        def _():
            outs[1][t, :m, :] = value

        return carry

    lax.fori_loop(begin, end, step, 0)
    copy_r.wait()
    norm_now = jnp.sum(r[...] * r[...], axis=0, keepdims=True)
    dir_norm = jnp.sum(d[...] * d[...], axis=0, keepdims=True)
    for ref in outs:
        for t in range(ref.shape[0]):
            ref[t, m:, :] = jnp.zeros((PAD, d.shape[1]), f32)
            ref[t, m : m + 1, :] = norm_now
            ref[t, m + 1 : m + 2, :] = dir_norm


def forward(inv_factor, direction, residual, chips, own):
    n, depth = inv_factor.shape
    t = direction.shape[1]
    m = n // chips // 2
    begin, end = (2 * chips - 1, 2 * chips) if own else (0, 2 * chips - 1)
    out = tuple(
        jax.ShapeDtypeStruct((count, m + PAD, t), f32)
        for count in ((1,) if own else (chips - 1, chips))
    )
    slots = 3
    far = pl.BlockSpec(memory_space=pl.ANY)
    return pl.pallas_call(
        functools.partial(forward_kernel, chips, begin, end, slots),
        in_specs=[far] * 3,
        out_specs=(local,) * len(out),
        out_shape=out,
        scratch_shapes=[
            pltpu.VMEM((slots, m, depth), f32),
            pltpu.SemaphoreType.DMA((slots,)),
            pltpu.VMEM((depth, t), f32),
            pltpu.VMEM((depth, t), f32),
            pltpu.VMEM((depth, 2 * t), bf16),
            pltpu.SemaphoreType.DMA((2,)),
        ],
        compiler_params=params(40),
        cost_estimate=cost(),
    )(*[pltpu.with_memory_space_constraint(x, pltpu.HBM) for x in (inv_factor, direction, residual)])


def add_kernel(n_terms, n_held, *refs):
    terms, outs = refs[:n_terms], refs[n_terms + n_held :]
    if len(outs) > 1 and len(terms[0].shape) == 3:
        outs[0][...] = terms[1][0]
        for i, out in enumerate(outs[1:]):
            out[...] = terms[0][i] + terms[1][i + 1]
        return
    value = terms[0][...]
    for term in terms[1:]:
        value += term[...]
    start = 0
    for out in outs:
        out[...] = value[start : start + out.shape[0], :]
        start += out.shape[0]


def add(terms, shapes, held=()):
    out = tuple(jax.ShapeDtypeStruct(shape, f32) for shape in shapes)
    return pl.pallas_call(
        functools.partial(add_kernel, len(terms), len(held)),
        in_specs=[local] * (len(terms) + len(held)),
        out_specs=(local,) * len(out),
        out_shape=out,
        compiler_params=params(),
        cost_estimate=cost(),
    )(*terms, *map(resident, held))


def cut_kernel(begin, x_ref, *refs):
    refs[-1][...] = x_ref[begin : begin + refs[-1].shape[0], :]


def cut(x, begin, rows, held=()):
    return pl.pallas_call(
        functools.partial(cut_kernel, begin),
        in_specs=[local] * (1 + len(held)),
        out_specs=local,
        out_shape=jax.ShapeDtypeStruct((rows, x.shape[1]), f32),
        compiler_params=params(),
        cost_estimate=cost(),
    )(x, *map(resident, held))


def kernel_kernel(segments, place, own_ref, other_ref, c_ref, high_ref, low_ref, ph, plo, psq):
    @pl.when(pl.program_id(0) == 0)
    def _():
        n = own_ref.shape[0]
        seg = n // segments
        for side, ref in enumerate((own_ref, other_ref)):
            for u in range(segments):
                start = pl.multiple_of((place[2] ^ u) * seg, seg)
                p = ref[pl.ds(start, seg), :]
                at = slice(side * n + u * seg, side * n + (u + 1) * seg)
                ph[at, :], plo[at, :] = split(p)
                psq[at, :] = jnp.broadcast_to(0.5 * jnp.sum(p * p, axis=1, keepdims=True), (seg, 128))

    c = c_ref[...]
    ch, cl = split(c)
    x = lax.dot_general(ch, ph[...], LAST, preferred_element_type=f32)
    x += lax.dot_general(ch, plo[...], LAST, preferred_element_type=f32)
    x += lax.dot_general(cl, ph[...], LAST, preferred_element_type=f32)
    center_sq = 0.5 * jnp.sum(c * c, axis=1, keepdims=True)
    point_sq = psq[...].T[0:1, :]
    high_ref[0], low_ref[0] = split(jnp.exp(x - (center_sq + point_sq)))


def gaussian(place, own, other, centers, chips, segments):
    n, width = own.shape
    m = centers.shape[0] // chips // 2
    out = jax.ShapeDtypeStruct((chips, m, 2 * n), bf16)
    block = pl.BlockSpec((1, m, 2 * n), lambda i, s: (i, 0, 0))
    return pl.pallas_call(
        functools.partial(kernel_kernel, segments),
        grid_spec=pltpu.PrefetchScalarGridSpec(
            num_scalar_prefetch=1,
            grid=(chips,),
            in_specs=[
                whole((n, width)),
                whole((n, width)),
                pl.BlockSpec((m, width), lambda i, s: (2 * (s[0] ^ i) + s[1], 0)),
            ],
            out_specs=(block, block),
            scratch_shapes=[
                pltpu.VMEM((2 * n, width), bf16),
                pltpu.VMEM((2 * n, width), bf16),
                pltpu.VMEM((2 * n, 128), f32),
            ],
        ),
        out_shape=(out, out),
        compiler_params=params(),
        cost_estimate=cost(12 * chips * m * n * width, 8 * chips * m * n, 2 * chips * m * n),
    )(place, own, other, pltpu.with_memory_space_constraint(centers, pltpu.HBM))


def predict_kernel(shift, begin, first, last, high_ref, low_ref, piece_ref, *refs):
    rows = slice(begin, begin + piece_ref.shape[0])
    value = turned(pair(piece_ref[...]), high_ref[shift, rows, :], low_ref[shift, rows, :])
    if not first:
        value += refs[0][...]
    if last:
        half = value.shape[1] // 2
        refs[-2][...] = value[:, :half].T
        refs[-1][...] = value[:, half:].T
    else:
        refs[-1][...] = value


def predict(shift, begin, high, low, piece, acc, last):
    _, m, n = high.shape
    t = piece.shape[1]
    args = [resident(high), resident(low), piece] + ([] if acc is None else [acc])
    if last:
        out = (jax.ShapeDtypeStruct((n // 2, t), f32),) * 2
    else:
        out = jax.ShapeDtypeStruct((t, n), f32)
    return pl.pallas_call(
        functools.partial(predict_kernel, shift, begin, acc is None, last),
        in_specs=[local] * len(args),
        out_specs=(local,) * 2 if last else local,
        out_shape=out,
        compiler_params=params(),
        cost_estimate=cost(8 * m * n * t, 4 * m * n),
    )(*args)


def back_kernel(shift, first, high_ref, low_ref, *refs):
    refs = refs[1:] if shift == 0 else refs
    if first:
        own_ref, other_ref, out_ref, pairs, norms = refs
        half = own_ref.shape[0]
        norms[...] = jnp.zeros_like(norms)
        a, b = own_ref[...], other_ref[...]
        pairs[:half, :] = pair(a)
        pairs[half:, :] = pair(b)
        norms[0:1, :] = jnp.sum(a * a, axis=0, keepdims=True) + jnp.sum(b * b, axis=0, keepdims=True)
    else:
        pairs, norms, out_ref = refs
    m = high_ref.shape[1]
    n = out_ref.shape[1]
    both = jnp.dot(high_ref[shift], pairs[...], preferred_element_type=f32)
    both += jnp.dot(low_ref[shift], pairs[...], preferred_element_type=f32)
    out_ref[:m, :] = both[:, :n] + both[:, n:]
    out_ref[m:, :] = norms[...]


def back_product(shift, high, low, sources, first, held=()):
    _, m, n = high.shape
    t = sources[1].shape[1]
    out = (jax.ShapeDtypeStruct((m + PAD, t), f32),)
    if first:
        out += (jax.ShapeDtypeStruct((n, 2 * t), bf16), jax.ShapeDtypeStruct((PAD, t), f32))
    return pl.pallas_call(
        functools.partial(back_kernel, shift, first),
        in_specs=[local] * (4 + len(held)),
        out_specs=(local,) * len(out),
        out_shape=out,
        compiler_params=params(),
        cost_estimate=cost(8 * m * n * t, 4 * m * n),
    )(resident(high), resident(low), *map(resident, held), *sources)


def transposed_kernel(m, shift, begin, sides, first, l_ref, *refs):
    chip, core, _ = here(2)
    pieces, refs = refs[: len(sides)], refs[len(sides) :]
    value = None if first else refs[0][...]
    for side, ref in zip(sides, pieces):
        n = ref.shape[0]
        step = min(n, 256)
        for i in range(0, n, step):
            start = pl.multiple_of(((chip ^ shift) * 2 + (core ^ side)) * m + begin + i, step)
            high, low = split(l_ref[pl.ds(start, step), :])
            share = turned(pair(ref[i : i + step, :]), high, low)
            value = share if value is None else value + share
    refs[-1][...] = value


def transposed(m, shift, begin, sides, inv_factor, pieces, acc):
    depth = inv_factor.shape[1]
    t = pieces[0].shape[1]
    args = [resident(inv_factor), *pieces] + ([] if acc is None else [acc])
    return pl.pallas_call(
        functools.partial(transposed_kernel, m, shift, begin, sides, acc is None),
        in_specs=[local] * len(args),
        out_specs=local,
        out_shape=jax.ShapeDtypeStruct((t, depth), f32),
        compiler_params=params(),
        cost_estimate=cost(),
    )(*args)


def last_kernel(m, places, part, segments, l_ref, acc_ref, *refs):
    pieces, (keep_ref, send_ref, image) = refs[: len(places)], refs[len(places) :]
    chip, core, segment = here(2 * segments)
    depth = acc_ref.shape[1]
    seg, n = depth // segments, image.shape[1]
    begin, end = cuts(seg)[part]
    bands = [(u * seg + begin, u * seg + end) for u in range(segments)]
    apart = all(edge % 128 == 0 for band in bands for edge in band)
    pairs = [pair(ref[...]) for ref in pieces]
    for u, (low_edge, high_edge) in enumerate(bands if apart else [(0, depth)]):
        value = acc_ref[:, low_edge:high_edge]
        for (shift, first), values in zip(places, pairs):
            count = values.shape[0]
            start = pl.multiple_of(((chip ^ shift) * 2 + 1 - core) * m + first, count)
            high, low = split(l_ref[pl.ds(start, count), low_edge:high_edge])
            value += turned(values, high, low)
        value = value.T
        if apart:
            image[u] = value
        else:
            for i, (first, final) in enumerate(bands):
                image[i] = value[first:final, :]
    half = segments // 2
    for u in range(segments):
        ref = keep_ref if u < half else send_ref
        ref[(u % half) * n : (u % half + 1) * n, :] = image[segment ^ u]


def last_transposed(m, part, segments, inv_factor, pieces, acc):
    t, depth = acc.shape
    begin, end = cuts(depth // segments)[part]
    out = jax.ShapeDtypeStruct((segments // 2 * (end - begin), t), f32)
    args = [resident(inv_factor), acc, *[piece for _, _, piece in pieces]]
    return pl.pallas_call(
        functools.partial(last_kernel, m, [piece[:2] for piece in pieces], part, segments),
        in_specs=[local] * len(args),
        out_specs=(local, local),
        out_shape=(out, out),
        scratch_shapes=[pltpu.VMEM((segments, end - begin, t), f32)],
        compiler_params=params(),
        cost_estimate=cost(),
    )(*args)


def update_kernel(begin, rows, segments, image_ref, r_ref, d_ref, pred_ref, norm_ref, *refs):
    new_ref, sum_ref = refs[-2:]
    norm_now, dir_norm = norm_ref[0:1, :], norm_ref[1:2, :]
    curvature = pred_ref[0:1, :] + ridge_weight * dir_norm
    step = norm_now / curvature
    start = here(2 * segments)[2] * rows + begin
    at = pl.ds(pl.multiple_of(start, PAD), image_ref.shape[0])
    new = r_ref[at, :] - step * (image_ref[...] + ridge_weight * d_ref[at, :])
    new_ref[...] = new
    total = jnp.broadcast_to(jnp.sum(new * new, axis=0, keepdims=True), sum_ref.shape)
    if len(refs) == 3:
        total += refs[0][...]
    sum_ref[...] = total


def update(begin, image, residual, direction, pred_norm, norms, before, segments):
    rows = residual.shape[0] // segments
    args = [image, residual, direction, pred_norm, norms] + ([] if before is None else [before])
    out = (jax.ShapeDtypeStruct(image.shape, f32), jax.ShapeDtypeStruct(norms.shape, f32))
    return pl.pallas_call(
        functools.partial(update_kernel, begin, rows, segments),
        in_specs=[local] * len(args),
        out_specs=(local, local),
        out_shape=out,
        compiler_params=params(),
        cost_estimate=cost(),
    )(*args)


def finish_kernel(segments, n_pieces, *refs):
    pieces = refs[:n_pieces]
    d_ref, norm_ref, next_ref, res_ref, dir_ref = refs[n_pieces:]
    ratio = next_ref[0:1, :] / norm_ref[0:1, :]
    segment = here(2 * segments)[2]
    seg = d_ref.shape[0] // segments
    each = n_pieces // len(SHARES)
    for c, (begin, end) in enumerate(cuts(seg)):
        n = end - begin
        u = 0
        for piece in pieces[c * each : (c + 1) * each]:
            for j in range(piece.shape[0] // n):
                at = pl.ds(pl.multiple_of((segment ^ u) * seg + begin, PAD), n)
                new = piece[j * n : (j + 1) * n, :]
                res_ref[at, :] = new
                dir_ref[at, :] = new + ratio * d_ref[at, :]
                u += 1


def finish(pieces, direction, norms, norm_next, segments):
    out = jax.ShapeDtypeStruct(direction.shape, f32)
    args = [*pieces, direction, norms, norm_next]
    return pl.pallas_call(
        functools.partial(finish_kernel, segments, len(pieces)),
        in_specs=[local] * len(args),
        out_specs=(local, local),
        out_shape=(out, out),
        compiler_params=params(),
        cost_estimate=cost(),
    )(*args)


def body(n_rows, n_cols, points, centers, inv_factor, solution, residual, direction):
    chips = n_rows // 2
    steps = n_cols.bit_length() - 1
    masks = [(2 << s) - 1 for s in range(steps)]
    halving, last_mask = masks[:-1], masks[-1]
    segments = n_cols // 2

    def swap(x, axis, mask):
        size = n_rows if axis == "rows" else n_cols
        return lax.ppermute(x, axis, [(i, i ^ mask) for i in range(size)])

    place = jnp.stack(here(n_cols)).astype(jnp.int32)
    order = list(range(1, chips))

    def gather(own, held=(), first=()):
        if chips != 4:
            return first, [(i, 0, swap(own, "rows", 2 * i)) for i in order]
        half = own.shape[0] // 2
        x, y = swap(own, "rows", 2), swap(own, "rows", 4)
        x, first = lax.optimization_barrier((x, first))
        through_y = swap(cut(x, half, half, held), "rows", 4)
        through_x = swap(cut(y, 0, half, held), "rows", 2)
        return first, [(1, 0, x), (2, 0, y), (3, half, through_y), (3, 0, through_x)]

    other_points = swap(points, "rows", 1)
    keep, send = forward(inv_factor, direction, residual, chips, False)
    m, t = send.shape[1] - PAD, send.shape[2]
    part, *totals = add([keep, swap(send, "rows", 1)], [(m + PAD, t)] * chips)
    got = [swap(totals[i - 1], "rows", 2 * i) for i in order]
    direction, part = lax.optimization_barrier((direction, part))
    (keep,) = forward(inv_factor, direction, residual, chips, True)
    mapped, norms = add([keep[0], part, *got], [(m, t), (PAD, t)])
    high, low = gaussian(place, points, other_points, centers, chips, segments)
    mapped, high, low = lax.optimization_barrier((mapped, high, low))

    arrived = [(0, 0, mapped), *gather(mapped)[1]]
    acc = None
    for j, (shift, begin, piece) in enumerate(arrived):
        acc = predict(shift, begin, high, low, piece, acc, j == len(arrived) - 1)
    keep, send = acc
    part = keep + swap(send, "rows", 1)
    for mask in halving:
        half = part.shape[0] // 2
        part = part[:half] + swap(part[half:], "cols", mask)
    part = part + swap(part, "cols", last_mask)
    for mask in halving[::-1]:
        part = jnp.concatenate([part, swap(part, "cols", mask)], axis=0)
    other = swap(part, "rows", 1)

    got = []
    sources, first = (part, other), True
    for shift in (*order, 0):
        piece, *rest = back_product(
            shift, high, low, sources, first, () if shift else (inv_factor,)
        )
        if first:
            sources, first = rest, False
        got.append(swap(piece, "rows", 2 * shift) if shift else piece)
    own, pred_norm = add([got[-1], *got[:-1]], [(m, t), (PAD, t)], (inv_factor,))

    acc = transposed(m, 0, 0, (0, 1), inv_factor, [own, swap(own, "rows", 1)], None)
    acc, arrived = gather(own, (inv_factor,), acc)
    late = []
    for shift, begin, piece in arrived:
        piece, acc = lax.optimization_barrier((piece, acc))
        late.append((shift, begin, swap(piece, "rows", 1)))
        acc = transposed(m, shift, begin, (0,), inv_factor, [piece], acc)
    pieces, norm_next, step_one, step_two, done = [], None, (), (), ()
    for c, (begin, _) in enumerate(cuts(residual.shape[0] // segments)):
        image, send = last_transposed(m, c, segments, inv_factor, late, acc)
        send, step_one = lax.optimization_barrier((send, step_one))
        step_one = swap(send, "cols", masks[0])
        image = image + step_one
        for mask in halving[1:]:
            half = image.shape[0] // 2
            image = image[:half] + swap(image[half:], "cols", mask)
        image, step_two = lax.optimization_barrier((image, step_two))
        step_two = swap(image, "cols", last_mask)
        image = image + step_two
        image, done = lax.optimization_barrier((image, done))
        new, norm_next = update(
            begin, image, residual, direction, pred_norm, norms, norm_next, segments
        )
        pieces.append(new)
        for mask in halving[::-1]:
            done = swap(new, "cols", mask)
            pieces.append(done)
            new = jnp.concatenate([new, done], axis=0)
    for mask in halving[::-1]:
        norm_next = norm_next + swap(norm_next, "cols", mask)
    norm_next = jnp.sum(lax.all_gather(norm_next, "rows"), axis=0)
    step = norms[0:1] / (pred_norm[0:1] + ridge_weight * norms[1:2])
    new_solution = solution + step * direction
    new_residual, new_direction = finish(
        pieces, direction, norms, norm_next, segments
    )
    return new_solution, new_residual, new_direction


def solution(mesh):
    return jax.shard_map(
        functools.partial(body, mesh.shape["rows"], mesh.shape["cols"]),
        mesh=mesh,
        in_specs=(
            P("rows", None),
            P("cols", None),
            P("cols", "rows"),
            P("rows", None),
            P("rows", None),
            P("rows", None),
        ),
        out_specs=(P("rows", None), P("rows", None), P("rows", None)),
        check_vma=False,
    )
```

```python
import functools

import jax
import jax.numpy as jnp
from jax import lax
from jax.experimental import pallas as pl
from jax.experimental.pallas import tpu as pltpu
from jax.sharding import PartitionSpec as P

ridge_weight = 0.02
PAD = 8
SHARES = (1, 3)
f32, bf16 = jnp.float32, jnp.bfloat16
FIRST = (((0,), (0,)), ((), ()))
LAST = (((1,), (1,)), ((), ()))


def split(value):
    high = value.astype(bf16)
    return high, (value - high.astype(f32)).astype(bf16)


def pair(value):
    high, low = split(value)
    return jnp.concatenate([high, low], axis=1)


def wide(lhs, pairs, dims=None):
    high, low = split(lhs)
    n = pairs.shape[1] // 2
    both = jnp.dot(high, pairs, preferred_element_type=f32)
    both += jnp.dot(low, pairs, preferred_element_type=f32)
    return both[:, :n] + both[:, n:]


def turned(pairs, high, low):
    n = pairs.shape[1] // 2
    both = lax.dot_general(pairs, high, FIRST, preferred_element_type=f32)
    both += lax.dot_general(pairs, low, FIRST, preferred_element_type=f32)
    return both[:n] + both[n:]


def params(mib=10):
    return pltpu.CompilerParams(vmem_limit_bytes=mib << 20)


def cost(*_):
    return pl.CostEstimate(flops=1, bytes_accessed=1, transcendentals=0)


local = pl.BlockSpec(memory_space=pltpu.VMEM)
scalars = pl.BlockSpec(memory_space=pltpu.SMEM)


def whole(shape):
    return pl.BlockSpec(shape, lambda *_: (0,) * len(shape))


def here(n_cols):
    row, col = lax.axis_index("rows"), lax.axis_index("cols")
    steps = n_cols.bit_length() - 1
    segment = 0
    for s in range(steps - 1):
        bit = ((col >> s) ^ (col >> (s + 1))) & 1
        segment = segment | (bit << (steps - 2 - s))
    return row >> 1, row & 1, segment


def cuts(rows):
    ends = [rows * sum(SHARES[: i + 1]) // sum(SHARES) for i in range(len(SHARES))]
    return list(zip([0, *ends], ends))


def resident(x):
    return pltpu.with_memory_space_constraint(x, pltpu.VMEM)


def forward_kernel(chips, begin, end, slots, l_ref, d_ref, r_ref, *refs):
    *outs, buffer, arrived, d, r, pairs, sems = refs
    m = buffer.shape[1]
    chip, core, _ = here(2)
    kept = chips - outs[0].shape[0] if begin == 0 else 0

    def job(n):
        return chips - 1 - (n >> 1), 1 - (n & 1)

    def copy(n):
        t, side = job(n)
        start = pl.multiple_of(((chip ^ t) * 2 + (core ^ side)) * m, m)
        slot = lax.rem(n, slots)
        return pltpu.make_async_copy(l_ref.at[pl.ds(start, m), :], buffer.at[slot], arrived.at[slot])

    copy_d = pltpu.make_async_copy(d_ref, d, sems.at[0])
    copy_r = pltpu.make_async_copy(r_ref, r, sems.at[1])
    copy_d.start()
    for n in range(begin, min(begin + slots - 1, end)):
        copy(n).start()
    copy_r.start()
    copy_d.wait()
    pairs[...] = pair(d[...])

    def step(n, carry):
        @pl.when(n + slots - 1 < end)
        def _():
            copy(n + slots - 1).start()

        copy(n).wait()
        value = wide(buffer[lax.rem(n, slots)], pairs[...])
        t, side = job(n)
        if begin:
            outs[0][t, :m, :] = value
            return carry

        @pl.when(side == 0)
        def _():
            outs[0][t - kept, :m, :] = value

        @pl.when(side == 1)
        def _():
            outs[1][t, :m, :] = value

        return carry

    lax.fori_loop(begin, end, step, 0)
    copy_r.wait()
    norm_now = jnp.sum(r[...] * r[...], axis=0, keepdims=True)
    dir_norm = jnp.sum(d[...] * d[...], axis=0, keepdims=True)
    for ref in outs:
        for t in range(ref.shape[0]):
            ref[t, m:, :] = jnp.zeros((PAD, d.shape[1]), f32)
            ref[t, m : m + 1, :] = norm_now
            ref[t, m + 1 : m + 2, :] = dir_norm


def forward(inv_factor, direction, residual, chips, own):
    n, depth = inv_factor.shape
    t = direction.shape[1]
    m = n // chips // 2
    begin, end = (2 * chips - 1, 2 * chips) if own else (0, 2 * chips - 1)
    out = tuple(
        jax.ShapeDtypeStruct((count, m + PAD, t), f32)
        for count in ((1,) if own else (chips - 1, chips))
    )
    slots = 3
    far = pl.BlockSpec(memory_space=pl.ANY)
    return pl.pallas_call(
        functools.partial(forward_kernel, chips, begin, end, slots),
        in_specs=[far] * 3,
        out_specs=(local,) * len(out),
        out_shape=out,
        scratch_shapes=[
            pltpu.VMEM((slots, m, depth), f32),
            pltpu.SemaphoreType.DMA((slots,)),
            pltpu.VMEM((depth, t), f32),
            pltpu.VMEM((depth, t), f32),
            pltpu.VMEM((depth, 2 * t), bf16),
            pltpu.SemaphoreType.DMA((2,)),
        ],
        compiler_params=params(40),
        cost_estimate=cost(),
    )(*[pltpu.with_memory_space_constraint(x, pltpu.HBM) for x in (inv_factor, direction, residual)])


def add_kernel(n_terms, n_held, *refs):
    terms, outs = refs[:n_terms], refs[n_terms + n_held :]
    if len(outs) > 1 and len(terms[0].shape) == 3:
        outs[0][...] = terms[1][0]
        for i, out in enumerate(outs[1:]):
            out[...] = terms[0][i] + terms[1][i + 1]
        return
    value = terms[0][...]
    for term in terms[1:]:
        value += term[...]
    start = 0
    for out in outs:
        out[...] = value[start : start + out.shape[0], :]
        start += out.shape[0]


def add(terms, shapes, held=()):
    out = tuple(jax.ShapeDtypeStruct(shape, f32) for shape in shapes)
    return pl.pallas_call(
        functools.partial(add_kernel, len(terms), len(held)),
        in_specs=[local] * (len(terms) + len(held)),
        out_specs=(local,) * len(out),
        out_shape=out,
        compiler_params=params(),
        cost_estimate=cost(),
    )(*terms, *map(resident, held))


def cut_kernel(begin, x_ref, *refs):
    refs[-1][...] = x_ref[begin : begin + refs[-1].shape[0], :]


def cut(x, begin, rows, held=()):
    return pl.pallas_call(
        functools.partial(cut_kernel, begin),
        in_specs=[local] * (1 + len(held)),
        out_specs=local,
        out_shape=jax.ShapeDtypeStruct((rows, x.shape[1]), f32),
        compiler_params=params(),
        cost_estimate=cost(),
    )(x, *map(resident, held))


def kernel_kernel(segments, place, own_ref, other_ref, c_ref, high_ref, low_ref, ph, plo, psq):
    @pl.when(pl.program_id(0) == 0)
    def _():
        n = own_ref.shape[0]
        seg = n // segments
        for side, ref in enumerate((own_ref, other_ref)):
            for u in range(segments):
                start = pl.multiple_of((place[2] ^ u) * seg, seg)
                p = ref[pl.ds(start, seg), :]
                at = slice(side * n + u * seg, side * n + (u + 1) * seg)
                ph[at, :], plo[at, :] = split(p)
                psq[at, :] = jnp.broadcast_to(0.5 * jnp.sum(p * p, axis=1, keepdims=True), (seg, 128))

    c = c_ref[...]
    ch, cl = split(c)
    x = lax.dot_general(ch, ph[...], LAST, preferred_element_type=f32)
    x += lax.dot_general(ch, plo[...], LAST, preferred_element_type=f32)
    x += lax.dot_general(cl, ph[...], LAST, preferred_element_type=f32)
    center_sq = 0.5 * jnp.sum(c * c, axis=1, keepdims=True)
    point_sq = psq[...].T[0:1, :]
    high_ref[0], low_ref[0] = split(jnp.exp(x - (center_sq + point_sq)))


def gaussian(place, own, other, centers, chips, segments):
    n, width = own.shape
    m = centers.shape[0] // chips // 2
    out = jax.ShapeDtypeStruct((chips, m, 2 * n), bf16)
    block = pl.BlockSpec((1, m, 2 * n), lambda i, s: (i, 0, 0))
    return pl.pallas_call(
        functools.partial(kernel_kernel, segments),
        grid_spec=pltpu.PrefetchScalarGridSpec(
            num_scalar_prefetch=1,
            grid=(chips,),
            in_specs=[
                whole((n, width)),
                whole((n, width)),
                pl.BlockSpec((m, width), lambda i, s: (2 * (s[0] ^ i) + s[1], 0)),
            ],
            out_specs=(block, block),
            scratch_shapes=[
                pltpu.VMEM((2 * n, width), bf16),
                pltpu.VMEM((2 * n, width), bf16),
                pltpu.VMEM((2 * n, 128), f32),
            ],
        ),
        out_shape=(out, out),
        compiler_params=params(),
        cost_estimate=cost(12 * chips * m * n * width, 8 * chips * m * n, 2 * chips * m * n),
    )(place, own, other, pltpu.with_memory_space_constraint(centers, pltpu.HBM))


def predict_kernel(shift, begin, first, last, high_ref, low_ref, piece_ref, *refs):
    rows = slice(begin, begin + piece_ref.shape[0])
    value = turned(pair(piece_ref[...]), high_ref[shift, rows, :], low_ref[shift, rows, :])
    if not first:
        value += refs[0][...]
    if last:
        half = value.shape[1] // 2
        refs[-2][...] = value[:, :half].T
        refs[-1][...] = value[:, half:].T
    else:
        refs[-1][...] = value


def predict(shift, begin, high, low, piece, acc, last):
    _, m, n = high.shape
    t = piece.shape[1]
    args = [resident(high), resident(low), piece] + ([] if acc is None else [acc])
    if last:
        out = (jax.ShapeDtypeStruct((n // 2, t), f32),) * 2
    else:
        out = jax.ShapeDtypeStruct((t, n), f32)
    return pl.pallas_call(
        functools.partial(predict_kernel, shift, begin, acc is None, last),
        in_specs=[local] * len(args),
        out_specs=(local,) * 2 if last else local,
        out_shape=out,
        compiler_params=params(),
        cost_estimate=cost(8 * m * n * t, 4 * m * n),
    )(*args)


def back_kernel(shifts, last, high_ref, low_ref, own_ref, *refs):
    half, n = own_ref.shape
    m = high_ref.shape[1]
    outs = refs[-len(shifts) :]
    begin = half if last else 0
    pairs = pair(refs[0][...] if last else own_ref[...])
    if last:
        norm = sum(
            jnp.sum(ref[...] * ref[...], axis=0, keepdims=True) for ref in (own_ref, refs[0])
        )
    for i, (shift, out_ref) in enumerate(zip(shifts, outs)):
        both = jnp.dot(high_ref[shift, :, begin : begin + half], pairs, preferred_element_type=f32)
        both += jnp.dot(low_ref[shift, :, begin : begin + half], pairs, preferred_element_type=f32)
        value = both[:, :n] + both[:, n:]
        if last:
            value += refs[1 + i][...]
            out_ref[m:, :] = jnp.zeros((PAD, n), f32)
            out_ref[m : m + 1, :] = norm
        out_ref[:m, :] = value


def back_product(shifts, high, low, own, other=None, before=(), held=()):
    m = high.shape[1]
    t = own.shape[1]
    last = other is not None
    args = [resident(high), resident(low), own, *([other] if last else []), *before]
    args += map(resident, held)
    out = (jax.ShapeDtypeStruct((m + PAD if last else m, t), f32),) * len(shifts)
    return pl.pallas_call(
        functools.partial(back_kernel, shifts, last),
        in_specs=[local] * len(args),
        out_specs=(local,) * len(out),
        out_shape=out,
        compiler_params=params(),
        cost_estimate=cost(),
    )(*args)


def transposed_kernel(m, shift, begin, sides, first, l_ref, *refs):
    chip, core, _ = here(2)
    pieces, refs = refs[: len(sides)], refs[len(sides) :]
    value = None if first else refs[0][...]
    for side, ref in zip(sides, pieces):
        n = ref.shape[0]
        step = min(n, 256)
        for i in range(0, n, step):
            start = pl.multiple_of(((chip ^ shift) * 2 + (core ^ side)) * m + begin + i, step)
            high, low = split(l_ref[pl.ds(start, step), :])
            share = turned(pair(ref[i : i + step, :]), high, low)
            value = share if value is None else value + share
    refs[-1][...] = value


def transposed(m, shift, begin, sides, inv_factor, pieces, acc):
    depth = inv_factor.shape[1]
    t = pieces[0].shape[1]
    args = [resident(inv_factor), *pieces] + ([] if acc is None else [acc])
    return pl.pallas_call(
        functools.partial(transposed_kernel, m, shift, begin, sides, acc is None),
        in_specs=[local] * len(args),
        out_specs=local,
        out_shape=jax.ShapeDtypeStruct((t, depth), f32),
        compiler_params=params(),
        cost_estimate=cost(),
    )(*args)


def last_kernel(m, places, part, segments, l_ref, acc_ref, *refs):
    pieces, (keep_ref, send_ref, image) = refs[: len(places)], refs[len(places) :]
    chip, core, segment = here(2 * segments)
    depth = acc_ref.shape[1]
    seg, n = depth // segments, image.shape[1]
    begin, end = cuts(seg)[part]
    bands = [(u * seg + begin, u * seg + end) for u in range(segments)]
    apart = all(edge % 128 == 0 for band in bands for edge in band)
    pairs = [pair(ref[...]) for ref in pieces]
    for u, (low_edge, high_edge) in enumerate(bands if apart else [(0, depth)]):
        value = acc_ref[:, low_edge:high_edge]
        for (shift, first), values in zip(places, pairs):
            count = values.shape[0]
            start = pl.multiple_of(((chip ^ shift) * 2 + 1 - core) * m + first, count)
            high, low = split(l_ref[pl.ds(start, count), low_edge:high_edge])
            value += turned(values, high, low)
        value = value.T
        if apart:
            image[u] = value
        else:
            for i, (first, final) in enumerate(bands):
                image[i] = value[first:final, :]
    half = segments // 2
    for u in range(segments):
        ref = keep_ref if u < half else send_ref
        ref[(u % half) * n : (u % half + 1) * n, :] = image[segment ^ u]


def last_transposed(m, part, segments, inv_factor, pieces, acc):
    t, depth = acc.shape
    begin, end = cuts(depth // segments)[part]
    out = jax.ShapeDtypeStruct((segments // 2 * (end - begin), t), f32)
    args = [resident(inv_factor), acc, *[piece for _, _, piece in pieces]]
    return pl.pallas_call(
        functools.partial(last_kernel, m, [piece[:2] for piece in pieces], part, segments),
        in_specs=[local] * len(args),
        out_specs=(local, local),
        out_shape=(out, out),
        scratch_shapes=[pltpu.VMEM((segments, end - begin, t), f32)],
        compiler_params=params(),
        cost_estimate=cost(),
    )(*args)


def update_kernel(begin, rows, segments, image_ref, r_ref, d_ref, pred_ref, norm_ref, *refs):
    new_ref, sum_ref = refs[-2:]
    norm_now, dir_norm = norm_ref[0:1, :], norm_ref[1:2, :]
    curvature = pred_ref[0:1, :] + ridge_weight * dir_norm
    step = norm_now / curvature
    start = here(2 * segments)[2] * rows + begin
    at = pl.ds(pl.multiple_of(start, PAD), image_ref.shape[0])
    new = r_ref[at, :] - step * (image_ref[...] + ridge_weight * d_ref[at, :])
    new_ref[...] = new
    total = jnp.broadcast_to(jnp.sum(new * new, axis=0, keepdims=True), sum_ref.shape)
    if len(refs) == 3:
        total += refs[0][...]
    sum_ref[...] = total


def update(begin, image, residual, direction, pred_norm, norms, before, segments):
    rows = residual.shape[0] // segments
    args = [image, residual, direction, pred_norm, norms] + ([] if before is None else [before])
    out = (jax.ShapeDtypeStruct(image.shape, f32), jax.ShapeDtypeStruct(norms.shape, f32))
    return pl.pallas_call(
        functools.partial(update_kernel, begin, rows, segments),
        in_specs=[local] * len(args),
        out_specs=(local, local),
        out_shape=out,
        compiler_params=params(),
        cost_estimate=cost(),
    )(*args)


def finish_kernel(segments, n_pieces, *refs):
    pieces = refs[:n_pieces]
    d_ref, norm_ref, next_ref, res_ref, dir_ref, new, sems = refs[n_pieces:]
    segment = here(2 * segments)[2]
    seg = d_ref.shape[0] // segments
    each = n_pieces // len(SHARES)
    places = []
    for c, (begin, end) in enumerate(cuts(seg)):
        u, n = 0, end - begin
        for piece in pieces[c * each : (c + 1) * each]:
            for j in range(piece.shape[0] // n):
                at = pl.ds(pl.multiple_of((segment ^ u) * seg + begin, PAD), n)
                places.append((piece.at[pl.ds(j * n, n), :], at))
                u += 1
    residuals = [
        pltpu.make_async_copy(rows, res_ref.at[at, :], sems.at[0, i])
        for i, (rows, at) in enumerate(places)
    ]
    directions = [
        pltpu.make_async_copy(new.at[at, :], dir_ref.at[at, :], sems.at[1, i])
        for i, (_, at) in enumerate(places)
    ]
    for copy in residuals:
        copy.start()
    ratio = next_ref[0:1, :] / norm_ref[0:1, :]
    for (rows, at), copy in zip(places, directions):
        new[at, :] = rows[...] + ratio * d_ref[at, :]
        copy.start()
    for copy in residuals + directions:
        copy.wait()


def finish(pieces, direction, norms, norm_next, segments):
    out = jax.ShapeDtypeStruct(direction.shape, f32)
    args = [*pieces, direction, norms, norm_next]
    far = pl.BlockSpec(memory_space=pl.ANY)
    return pl.pallas_call(
        functools.partial(finish_kernel, segments, len(pieces)),
        in_specs=[local] * len(args),
        out_specs=(far, far),
        out_shape=(out, out),
        scratch_shapes=[
            pltpu.VMEM(direction.shape, f32),
            pltpu.SemaphoreType.DMA((2, segments * len(SHARES))),
        ],
        compiler_params=params(),
        cost_estimate=cost(),
    )(*args)


def body(n_rows, n_cols, points, centers, inv_factor, solution, residual, direction):
    chips = n_rows // 2
    steps = n_cols.bit_length() - 1
    masks = [(2 << s) - 1 for s in range(steps)]
    halving, last_mask = masks[:-1], masks[-1]
    segments = n_cols // 2

    def swap(x, axis, mask):
        size = n_rows if axis == "rows" else n_cols
        return lax.ppermute(x, axis, [(i, i ^ mask) for i in range(size)])

    place = jnp.stack(here(n_cols)).astype(jnp.int32)
    order = list(range(1, chips))

    def gather(own, held=(), first=()):
        if chips != 4:
            return first, [(i, 0, swap(own, "rows", 2 * i)) for i in order]
        half = own.shape[0] // 2
        x, y = swap(own, "rows", 2), swap(own, "rows", 4)
        x, first = lax.optimization_barrier((x, first))
        through_y = swap(cut(x, half, half, held), "rows", 4)
        through_x = swap(cut(y, 0, half, held), "rows", 2)
        return first, [(1, 0, x), (2, 0, y), (3, half, through_y), (3, 0, through_x)]

    other_points = swap(points, "rows", 1)
    keep, send = forward(inv_factor, direction, residual, chips, False)
    m, t = send.shape[1] - PAD, send.shape[2]
    part, *totals = add([keep, swap(send, "rows", 1)], [(m + PAD, t)] * chips)
    got = [swap(totals[i - 1], "rows", 2 * i) for i in order]
    direction, part = lax.optimization_barrier((direction, part))
    (keep,) = forward(inv_factor, direction, residual, chips, True)
    mapped, norms = add([keep[0], part, *got], [(m, t), (PAD, t)])
    high, low = gaussian(place, points, other_points, centers, chips, segments)
    mapped, high, low = lax.optimization_barrier((mapped, high, low))

    arrived = [(0, 0, mapped), *gather(mapped)[1]]
    acc = None
    for j, (shift, begin, piece) in enumerate(arrived):
        acc = predict(shift, begin, high, low, piece, acc, j == len(arrived) - 1)
    keep, send = acc
    part = keep + swap(send, "rows", 1)
    for mask in halving:
        half = part.shape[0] // 2
        part = part[:half] + swap(part[half:], "cols", mask)
    part = part + swap(part, "cols", last_mask)
    for mask in halving[::-1]:
        part = jnp.concatenate([part, swap(part, "cols", mask)], axis=0)
    before = back_product((*order, 0), high, low, part)
    other = swap(part, "rows", 1)
    pieces = back_product(order, high, low, part, other, before[:-1])
    got = [swap(piece, "rows", 2 * i) for i, piece in zip(order, pieces)]
    got += back_product((0,), high, low, part, other, before[-1:], (inv_factor,))
    own, pred_norm = add([got[-1], *got[:-1]], [(m, t), (PAD, t)], (inv_factor,))

    acc = transposed(m, 0, 0, (0, 1), inv_factor, [own, swap(own, "rows", 1)], None)
    acc, arrived = gather(own, (inv_factor,), acc)
    late = []
    for shift, begin, piece in arrived:
        piece, acc = lax.optimization_barrier((piece, acc))
        late.append((shift, begin, swap(piece, "rows", 1)))
        acc = transposed(m, shift, begin, (0,), inv_factor, [piece], acc)
    pieces, norm_next, step_one, step_two, done = [], None, (), (), ()
    for c, (begin, _) in enumerate(cuts(residual.shape[0] // segments)):
        image, send = last_transposed(m, c, segments, inv_factor, late, acc)
        send, step_one = lax.optimization_barrier((send, step_one))
        step_one = swap(send, "cols", masks[0])
        image = image + step_one
        for mask in halving[1:]:
            half = image.shape[0] // 2
            image = image[:half] + swap(image[half:], "cols", mask)
        image, step_two = lax.optimization_barrier((image, step_two))
        step_two = swap(image, "cols", last_mask)
        image = image + step_two
        image, done = lax.optimization_barrier((image, done))
        new, norm_next = update(
            begin, image, residual, direction, pred_norm, norms, norm_next, segments
        )
        pieces.append(new)
        for mask in halving[::-1]:
            done = swap(new, "cols", mask)
            pieces.append(done)
            new = jnp.concatenate([new, done], axis=0)
    for mask in halving[::-1]:
        norm_next = norm_next + swap(norm_next, "cols", mask)
    norm_next = jnp.sum(lax.all_gather(norm_next, "rows"), axis=0)
    step = norms[0:1] / (pred_norm[0:1] + ridge_weight * norms[1:2])
    new_solution = solution + step * direction
    new_residual, new_direction = finish(
        pieces, direction, norms, norm_next, segments
    )
    return new_solution, new_residual, new_direction


def solution(mesh):
    return jax.shard_map(
        functools.partial(body, mesh.shape["rows"], mesh.shape["cols"]),
        mesh=mesh,
        in_specs=(
            P("rows", None),
            P("cols", None),
            P("cols", "rows"),
            P("rows", None),
            P("rows", None),
            P("rows", None),
        ),
        out_specs=(P("rows", None), P("rows", None), P("rows", None)),
        check_vma=False,
    )
```

```python
import functools

import jax
import jax.numpy as jnp
from jax import lax
from jax.experimental import pallas as pl
from jax.experimental.pallas import tpu as pltpu
from jax.sharding import PartitionSpec as P

ridge_weight = 0.02
PAD = 8
SHARES = (1, 3)
f32, bf16 = jnp.float32, jnp.bfloat16
FIRST = (((0,), (0,)), ((), ()))
LAST = (((1,), (1,)), ((), ()))


def split(value):
    high = value.astype(bf16)
    return high, (value - high.astype(f32)).astype(bf16)


def pair(value):
    high, low = split(value)
    return jnp.concatenate([high, low], axis=1)


def wide(lhs, pairs, dims=None):
    high, low = split(lhs)
    n = pairs.shape[1] // 2
    both = jnp.dot(high, pairs, preferred_element_type=f32)
    both += jnp.dot(low, pairs, preferred_element_type=f32)
    return both[:, :n] + both[:, n:]


def turned(pairs, high, low):
    n = pairs.shape[1] // 2
    both = lax.dot_general(pairs, high, FIRST, preferred_element_type=f32)
    both += lax.dot_general(pairs, low, FIRST, preferred_element_type=f32)
    return both[:n] + both[n:]


def params(mib=10):
    return pltpu.CompilerParams(vmem_limit_bytes=mib << 20)


def cost(*_):
    return pl.CostEstimate(flops=1, bytes_accessed=1, transcendentals=0)


local = pl.BlockSpec(memory_space=pltpu.VMEM)
scalars = pl.BlockSpec(memory_space=pltpu.SMEM)


def whole(shape):
    return pl.BlockSpec(shape, lambda *_: (0,) * len(shape))


def here(n_cols):
    row, col = lax.axis_index("rows"), lax.axis_index("cols")
    steps = n_cols.bit_length() - 1
    segment = 0
    for s in range(steps - 1):
        bit = ((col >> s) ^ (col >> (s + 1))) & 1
        segment = segment | (bit << (steps - 2 - s))
    return row >> 1, row & 1, segment


def cuts(rows):
    ends = [rows * sum(SHARES[: i + 1]) // sum(SHARES) for i in range(len(SHARES))]
    return list(zip([0, *ends], ends))


def resident(x):
    return pltpu.with_memory_space_constraint(x, pltpu.VMEM)


def forward_kernel(chips, begin, end, slots, l_ref, d_ref, r_ref, *refs):
    *outs, buffer, arrived, d, r, pairs, sems = refs
    m = buffer.shape[1]
    chip, core, _ = here(2)
    kept = chips - outs[0].shape[0] if begin == 0 else 0

    def job(n):
        return chips - 1 - (n >> 1), 1 - (n & 1)

    def copy(n):
        t, side = job(n)
        start = pl.multiple_of(((chip ^ t) * 2 + (core ^ side)) * m, m)
        slot = lax.rem(n, slots)
        return pltpu.make_async_copy(l_ref.at[pl.ds(start, m), :], buffer.at[slot], arrived.at[slot])

    copy_d = pltpu.make_async_copy(d_ref, d, sems.at[0])
    copy_r = pltpu.make_async_copy(r_ref, r, sems.at[1])
    copy_d.start()
    for n in range(begin, min(begin + slots - 1, end)):
        copy(n).start()
    copy_r.start()
    copy_d.wait()
    pairs[...] = pair(d[...])

    def step(n, carry):
        @pl.when(n + slots - 1 < end)
        def _():
            copy(n + slots - 1).start()

        copy(n).wait()
        value = wide(buffer[lax.rem(n, slots)], pairs[...])
        t, side = job(n)
        if begin:
            outs[0][t, :m, :] = value
            return carry

        @pl.when(side == 0)
        def _():
            outs[0][t - kept, :m, :] = value

        @pl.when(side == 1)
        def _():
            outs[1][t, :m, :] = value

        return carry

    lax.fori_loop(begin, end, step, 0)
    copy_r.wait()
    norm_now = jnp.sum(r[...] * r[...], axis=0, keepdims=True)
    dir_norm = jnp.sum(d[...] * d[...], axis=0, keepdims=True)
    for ref in outs:
        for t in range(ref.shape[0]):
            ref[t, m:, :] = jnp.zeros((PAD, d.shape[1]), f32)
            ref[t, m : m + 1, :] = norm_now
            ref[t, m + 1 : m + 2, :] = dir_norm


def forward(inv_factor, direction, residual, chips, own):
    n, depth = inv_factor.shape
    t = direction.shape[1]
    m = n // chips // 2
    begin, end = (2 * chips - 1, 2 * chips) if own else (0, 2 * chips - 1)
    out = tuple(
        jax.ShapeDtypeStruct((count, m + PAD, t), f32)
        for count in ((1,) if own else (chips - 1, chips))
    )
    slots = 4
    far = pl.BlockSpec(memory_space=pl.ANY)
    return pl.pallas_call(
        functools.partial(forward_kernel, chips, begin, end, slots),
        in_specs=[far] * 3,
        out_specs=(local,) * len(out),
        out_shape=out,
        scratch_shapes=[
            pltpu.VMEM((slots, m, depth), f32),
            pltpu.SemaphoreType.DMA((slots,)),
            pltpu.VMEM((depth, t), f32),
            pltpu.VMEM((depth, t), f32),
            pltpu.VMEM((depth, 2 * t), bf16),
            pltpu.SemaphoreType.DMA((2,)),
        ],
        compiler_params=params(40),
        cost_estimate=cost(),
    )(*[pltpu.with_memory_space_constraint(x, pltpu.HBM) for x in (inv_factor, direction, residual)])


def add_kernel(n_terms, n_held, *refs):
    terms, outs = refs[:n_terms], refs[n_terms + n_held :]
    if len(outs) > 1 and len(terms[0].shape) == 3:
        outs[0][...] = terms[1][0]
        for i, out in enumerate(outs[1:]):
            out[...] = terms[0][i] + terms[1][i + 1]
        return
    value = terms[0][...]
    for term in terms[1:]:
        value += term[...]
    start = 0
    for out in outs:
        out[...] = value[start : start + out.shape[0], :]
        start += out.shape[0]


def add(terms, shapes, held=()):
    out = tuple(jax.ShapeDtypeStruct(shape, f32) for shape in shapes)
    return pl.pallas_call(
        functools.partial(add_kernel, len(terms), len(held)),
        in_specs=[local] * (len(terms) + len(held)),
        out_specs=(local,) * len(out),
        out_shape=out,
        compiler_params=params(),
        cost_estimate=cost(),
    )(*terms, *map(resident, held))


def cut_kernel(begin, x_ref, *refs):
    refs[-1][...] = x_ref[begin : begin + refs[-1].shape[0], :]


def cut(x, begin, rows, held=()):
    return pl.pallas_call(
        functools.partial(cut_kernel, begin),
        in_specs=[local] * (1 + len(held)),
        out_specs=local,
        out_shape=jax.ShapeDtypeStruct((rows, x.shape[1]), f32),
        compiler_params=params(),
        cost_estimate=cost(),
    )(x, *map(resident, held))


def kernel_kernel(segments, place, own_ref, other_ref, c_ref, high_ref, low_ref, ph, plo, psq):
    @pl.when(pl.program_id(0) == 0)
    def _():
        n = own_ref.shape[0]
        seg = n // segments
        for side, ref in enumerate((own_ref, other_ref)):
            for u in range(segments):
                start = pl.multiple_of((place[2] ^ u) * seg, seg)
                p = ref[pl.ds(start, seg), :]
                at = slice(side * n + u * seg, side * n + (u + 1) * seg)
                ph[at, :], plo[at, :] = split(p)
                psq[at, :] = jnp.broadcast_to(0.5 * jnp.sum(p * p, axis=1, keepdims=True), (seg, 128))

    c = c_ref[...]
    ch, cl = split(c)
    x = lax.dot_general(ch, ph[...], LAST, preferred_element_type=f32)
    x += lax.dot_general(ch, plo[...], LAST, preferred_element_type=f32)
    x += lax.dot_general(cl, ph[...], LAST, preferred_element_type=f32)
    center_sq = 0.5 * jnp.sum(c * c, axis=1, keepdims=True)
    point_sq = psq[...].T[0:1, :]
    high_ref[0], low_ref[0] = split(jnp.exp(x - (center_sq + point_sq)))


def gaussian(place, own, other, centers, chips, segments):
    n, width = own.shape
    m = centers.shape[0] // chips // 2
    out = jax.ShapeDtypeStruct((chips, m, 2 * n), bf16)
    block = pl.BlockSpec((1, m, 2 * n), lambda i, s: (i, 0, 0))
    return pl.pallas_call(
        functools.partial(kernel_kernel, segments),
        grid_spec=pltpu.PrefetchScalarGridSpec(
            num_scalar_prefetch=1,
            grid=(chips,),
            in_specs=[
                whole((n, width)),
                whole((n, width)),
                pl.BlockSpec((m, width), lambda i, s: (2 * (s[0] ^ i) + s[1], 0)),
            ],
            out_specs=(block, block),
            scratch_shapes=[
                pltpu.VMEM((2 * n, width), bf16),
                pltpu.VMEM((2 * n, width), bf16),
                pltpu.VMEM((2 * n, 128), f32),
            ],
        ),
        out_shape=(out, out),
        compiler_params=params(),
        cost_estimate=cost(12 * chips * m * n * width, 8 * chips * m * n, 2 * chips * m * n),
    )(place, own, other, pltpu.with_memory_space_constraint(centers, pltpu.HBM))


def predict_kernel(shift, begin, first, last, high_ref, low_ref, piece_ref, *refs):
    rows = slice(begin, begin + piece_ref.shape[0])
    value = turned(pair(piece_ref[...]), high_ref[shift, rows, :], low_ref[shift, rows, :])
    if not first:
        value += refs[0][...]
    if last:
        half = value.shape[1] // 2
        refs[-2][...] = value[:, :half].T
        refs[-1][...] = value[:, half:].T
    else:
        refs[-1][...] = value


def predict(shift, begin, high, low, piece, acc, last):
    _, m, n = high.shape
    t = piece.shape[1]
    args = [resident(high), resident(low), piece] + ([] if acc is None else [acc])
    if last:
        out = (jax.ShapeDtypeStruct((n // 2, t), f32),) * 2
    else:
        out = jax.ShapeDtypeStruct((t, n), f32)
    return pl.pallas_call(
        functools.partial(predict_kernel, shift, begin, acc is None, last),
        in_specs=[local] * len(args),
        out_specs=(local,) * 2 if last else local,
        out_shape=out,
        compiler_params=params(),
        cost_estimate=cost(8 * m * n * t, 4 * m * n),
    )(*args)


def back_kernel(shifts, last, high_ref, low_ref, own_ref, *refs):
    half, n = own_ref.shape
    m = high_ref.shape[1]
    outs = refs[-len(shifts) :]
    begin = half if last else 0
    pairs = pair(refs[0][...] if last else own_ref[...])
    if last:
        norm = sum(
            jnp.sum(ref[...] * ref[...], axis=0, keepdims=True) for ref in (own_ref, refs[0])
        )
    for i, (shift, out_ref) in enumerate(zip(shifts, outs)):
        both = jnp.dot(high_ref[shift, :, begin : begin + half], pairs, preferred_element_type=f32)
        both += jnp.dot(low_ref[shift, :, begin : begin + half], pairs, preferred_element_type=f32)
        value = both[:, :n] + both[:, n:]
        if last:
            value += refs[1 + i][...]
            out_ref[m:, :] = jnp.zeros((PAD, n), f32)
            out_ref[m : m + 1, :] = norm
        out_ref[:m, :] = value


def back_product(shifts, high, low, own, other=None, before=(), held=()):
    m = high.shape[1]
    t = own.shape[1]
    last = other is not None
    args = [resident(high), resident(low), own, *([other] if last else []), *before]
    args += map(resident, held)
    out = (jax.ShapeDtypeStruct((m + PAD if last else m, t), f32),) * len(shifts)
    return pl.pallas_call(
        functools.partial(back_kernel, shifts, last),
        in_specs=[local] * len(args),
        out_specs=(local,) * len(out),
        out_shape=out,
        compiler_params=params(),
        cost_estimate=cost(),
    )(*args)


def transposed_kernel(m, places, first, l_ref, *refs):
    chip, core, _ = here(2)
    pieces, refs = refs[: len(places)], refs[len(places) :]
    value = None if first else refs[0][...]
    for (shift, begin, side), ref in zip(places, pieces):
        n = ref.shape[0]
        step = min(n, 256)
        for i in range(0, n, step):
            start = pl.multiple_of(((chip ^ shift) * 2 + (core ^ side)) * m + begin + i, step)
            high, low = split(l_ref[pl.ds(start, step), :])
            share = turned(pair(ref[i : i + step, :]), high, low)
            value = share if value is None else value + share
    refs[-1][...] = value


def transposed(m, places, inv_factor, pieces, acc):
    depth = inv_factor.shape[1]
    t = pieces[0].shape[1]
    args = [resident(inv_factor), *pieces] + ([] if acc is None else [acc])
    return pl.pallas_call(
        functools.partial(transposed_kernel, m, places, acc is None),
        in_specs=[local] * len(args),
        out_specs=local,
        out_shape=jax.ShapeDtypeStruct((t, depth), f32),
        compiler_params=params(),
        cost_estimate=cost(),
    )(*args)


def last_kernel(m, places, part, segments, l_ref, acc_ref, *refs):
    pieces, (keep_ref, send_ref, image) = refs[: len(places)], refs[len(places) :]
    chip, core, segment = here(2 * segments)
    depth = acc_ref.shape[1]
    seg, n = depth // segments, image.shape[1]
    begin, end = cuts(seg)[part]
    bands = [(u * seg + begin, u * seg + end) for u in range(segments)]
    apart = all(edge % 128 == 0 for band in bands for edge in band)
    pairs = [pair(ref[...]) for ref in pieces]
    for u, (low_edge, high_edge) in enumerate(bands if apart else [(0, depth)]):
        value = acc_ref[:, low_edge:high_edge]
        for (shift, first), values in zip(places, pairs):
            count = values.shape[0]
            start = pl.multiple_of(((chip ^ shift) * 2 + 1 - core) * m + first, count)
            high, low = split(l_ref[pl.ds(start, count), low_edge:high_edge])
            value += turned(values, high, low)
        value = value.T
        if apart:
            image[u] = value
        else:
            for i, (first, final) in enumerate(bands):
                image[i] = value[first:final, :]
    half = segments // 2
    for u in range(segments):
        ref = keep_ref if u < half else send_ref
        ref[(u % half) * n : (u % half + 1) * n, :] = image[segment ^ u]


def last_transposed(m, part, segments, inv_factor, pieces, acc):
    t, depth = acc.shape
    begin, end = cuts(depth // segments)[part]
    out = jax.ShapeDtypeStruct((segments // 2 * (end - begin), t), f32)
    args = [resident(inv_factor), acc, *[piece for _, _, piece in pieces]]
    return pl.pallas_call(
        functools.partial(last_kernel, m, [piece[:2] for piece in pieces], part, segments),
        in_specs=[local] * len(args),
        out_specs=(local, local),
        out_shape=(out, out),
        scratch_shapes=[pltpu.VMEM((segments, end - begin, t), f32)],
        compiler_params=params(),
        cost_estimate=cost(),
    )(*args)


def update_kernel(begin, rows, segments, image_ref, r_ref, d_ref, pred_ref, norm_ref, *refs):
    new_ref, sum_ref = refs[-2:]
    norm_now, dir_norm = norm_ref[0:1, :], norm_ref[1:2, :]
    curvature = pred_ref[0:1, :] + ridge_weight * dir_norm
    step = norm_now / curvature
    start = here(2 * segments)[2] * rows + begin
    at = pl.ds(pl.multiple_of(start, PAD), image_ref.shape[0])
    new = r_ref[at, :] - step * (image_ref[...] + ridge_weight * d_ref[at, :])
    new_ref[...] = new
    total = jnp.broadcast_to(jnp.sum(new * new, axis=0, keepdims=True), sum_ref.shape)
    if len(refs) == 3:
        total += refs[0][...]
    sum_ref[...] = total


def update(begin, image, residual, direction, pred_norm, norms, before, segments):
    rows = residual.shape[0] // segments
    args = [image, residual, direction, pred_norm, norms] + ([] if before is None else [before])
    out = (jax.ShapeDtypeStruct(image.shape, f32), jax.ShapeDtypeStruct(norms.shape, f32))
    return pl.pallas_call(
        functools.partial(update_kernel, begin, rows, segments),
        in_specs=[local] * len(args),
        out_specs=(local, local),
        out_shape=out,
        compiler_params=params(),
        cost_estimate=cost(),
    )(*args)


def finish_kernel(segments, n_pieces, *refs):
    pieces = refs[:n_pieces]
    d_ref, norm_ref, next_ref, res_ref, dir_ref, new, sems = refs[n_pieces:]
    segment = here(2 * segments)[2]
    seg = d_ref.shape[0] // segments
    each = n_pieces // len(SHARES)
    places = []
    for c, (begin, end) in enumerate(cuts(seg)):
        u, n = 0, end - begin
        for piece in pieces[c * each : (c + 1) * each]:
            for j in range(piece.shape[0] // n):
                at = pl.ds(pl.multiple_of((segment ^ u) * seg + begin, PAD), n)
                places.append((piece.at[pl.ds(j * n, n), :], at))
                u += 1
    residuals = [
        pltpu.make_async_copy(rows, res_ref.at[at, :], sems.at[0, i])
        for i, (rows, at) in enumerate(places)
    ]
    directions = [
        pltpu.make_async_copy(new.at[at, :], dir_ref.at[at, :], sems.at[1, i])
        for i, (_, at) in enumerate(places)
    ]
    for copy in residuals:
        copy.start()
    ratio = next_ref[0:1, :] / norm_ref[0:1, :]
    for (rows, at), copy in zip(places, directions):
        new[at, :] = rows[...] + ratio * d_ref[at, :]
        copy.start()
    for copy in residuals + directions:
        copy.wait()


def finish(pieces, direction, norms, norm_next, segments):
    out = jax.ShapeDtypeStruct(direction.shape, f32)
    args = [*pieces, direction, norms, norm_next]
    far = pl.BlockSpec(memory_space=pl.ANY)
    return pl.pallas_call(
        functools.partial(finish_kernel, segments, len(pieces)),
        in_specs=[local] * len(args),
        out_specs=(far, far),
        out_shape=(out, out),
        scratch_shapes=[
            pltpu.VMEM(direction.shape, f32),
            pltpu.SemaphoreType.DMA((2, segments * len(SHARES))),
        ],
        compiler_params=params(),
        cost_estimate=cost(),
    )(*args)


def body(n_rows, n_cols, points, centers, inv_factor, solution, residual, direction):
    chips = n_rows // 2
    steps = n_cols.bit_length() - 1
    masks = [(2 << s) - 1 for s in range(steps)]
    halving, last_mask = masks[:-1], masks[-1]
    segments = n_cols // 2

    def swap(x, axis, mask):
        size = n_rows if axis == "rows" else n_cols
        return lax.ppermute(x, axis, [(i, i ^ mask) for i in range(size)])

    place = jnp.stack(here(n_cols)).astype(jnp.int32)
    order = list(range(1, chips))

    def gather(own, held=(), first=()):
        if chips != 4:
            return first, [(i, 0, swap(own, "rows", 2 * i)) for i in order]
        half = own.shape[0] // 2
        x, y = swap(own, "rows", 2), swap(own, "rows", 4)
        x, first = lax.optimization_barrier((x, first))
        through_y = swap(cut(x, half, half, held), "rows", 4)
        through_x = swap(cut(y, 0, half, held), "rows", 2)
        return first, [(1, 0, x), (2, 0, y), (3, half, through_y), (3, 0, through_x)]

    other_points = swap(points, "rows", 1)
    keep, send = forward(inv_factor, direction, residual, chips, False)
    m, t = send.shape[1] - PAD, send.shape[2]
    part, *totals = add([keep, swap(send, "rows", 1)], [(m + PAD, t)] * chips)
    got = [swap(totals[i - 1], "rows", 2 * i) for i in order]
    direction, part = lax.optimization_barrier((direction, part))
    (keep,) = forward(inv_factor, direction, residual, chips, True)
    mapped, norms = add([keep[0], part, *got], [(m, t), (PAD, t)])
    high, low = gaussian(place, points, other_points, centers, chips, segments)
    mapped, high, low = lax.optimization_barrier((mapped, high, low))

    arrived = [(0, 0, mapped), *gather(mapped)[1]]
    acc = None
    for j, (shift, begin, piece) in enumerate(arrived):
        acc = predict(shift, begin, high, low, piece, acc, j == len(arrived) - 1)
    keep, send = acc
    part = keep + swap(send, "rows", 1)
    for mask in halving:
        half = part.shape[0] // 2
        part = part[:half] + swap(part[half:], "cols", mask)
    part = part + swap(part, "cols", last_mask)
    for mask in halving[::-1]:
        part = jnp.concatenate([part, swap(part, "cols", mask)], axis=0)
    before = back_product((*order, 0), high, low, part)
    other = swap(part, "rows", 1)
    pieces = back_product(order, high, low, part, other, before[:-1])
    got = [swap(piece, "rows", 2 * i) for i, piece in zip(order, pieces)]
    got += back_product((0,), high, low, part, other, before[-1:], (inv_factor,))
    own, pred_norm = add([got[-1], *got[:-1]], [(m, t), (PAD, t)], (inv_factor,))

    acc = transposed(m, [(0, 0, 0), (0, 0, 1)], inv_factor, [own, swap(own, "rows", 1)], None)
    acc, arrived = gather(own, (inv_factor,), acc)
    late = []
    turns = [arrived[:2], *([one] for one in arrived[2:])]
    for turn in turns:
        pieces, acc = lax.optimization_barrier(([one[2] for one in turn], acc))
        places = [(shift, begin, 0) for shift, begin, _ in turn]
        late += [(*one[:2], swap(piece, "rows", 1)) for one, piece in zip(turn, pieces)]
        acc = transposed(m, places, inv_factor, pieces, acc)
    pieces, norm_next, step_one, step_two, done = [], None, (), (), ()
    for c, (begin, _) in enumerate(cuts(residual.shape[0] // segments)):
        image, send = last_transposed(m, c, segments, inv_factor, late, acc)
        send, step_one = lax.optimization_barrier((send, step_one))
        step_one = swap(send, "cols", masks[0])
        image = image + step_one
        for mask in halving[1:]:
            half = image.shape[0] // 2
            image = image[:half] + swap(image[half:], "cols", mask)
        image, step_two = lax.optimization_barrier((image, step_two))
        step_two = swap(image, "cols", last_mask)
        image = image + step_two
        image, done = lax.optimization_barrier((image, done))
        new, norm_next = update(
            begin, image, residual, direction, pred_norm, norms, norm_next, segments
        )
        pieces.append(new)
        for mask in halving[::-1]:
            done = swap(new, "cols", mask)
            pieces.append(done)
            new = jnp.concatenate([new, done], axis=0)
    for mask in halving[::-1]:
        norm_next = norm_next + swap(norm_next, "cols", mask)
    norm_next = jnp.sum(lax.all_gather(norm_next, "rows"), axis=0)
    step = norms[0:1] / (pred_norm[0:1] + ridge_weight * norms[1:2])
    new_solution = solution + step * direction
    new_residual, new_direction = finish(
        pieces, direction, norms, norm_next, segments
    )
    return new_solution, new_residual, new_direction


def solution(mesh):
    return jax.shard_map(
        functools.partial(body, mesh.shape["rows"], mesh.shape["cols"]),
        mesh=mesh,
        in_specs=(
            P("rows", None),
            P("cols", None),
            P("cols", "rows"),
            P("rows", None),
            P("rows", None),
            P("rows", None),
        ),
        out_specs=(P("rows", None), P("rows", None), P("rows", None)),
        check_vma=False,
    )
```

```python
import functools

import jax
import jax.numpy as jnp
from jax import lax
from jax.experimental import pallas as pl
from jax.experimental.pallas import tpu as pltpu
from jax.sharding import PartitionSpec as P

ridge_weight = 0.02
PAD = 8
SHARES = (1, 3)
f32, bf16 = jnp.float32, jnp.bfloat16
FIRST = (((0,), (0,)), ((), ()))
LAST = (((1,), (1,)), ((), ()))


def split(value):
    high = value.astype(bf16)
    return high, (value - high.astype(f32)).astype(bf16)


def pair(value):
    high, low = split(value)
    return jnp.concatenate([high, low], axis=1)


def wide(lhs, pairs, dims=None):
    high, low = split(lhs)
    n = pairs.shape[1] // 2
    both = jnp.dot(high, pairs, preferred_element_type=f32)
    both += jnp.dot(low, pairs, preferred_element_type=f32)
    return both[:, :n] + both[:, n:]


def turned(pairs, high, low):
    n = pairs.shape[1] // 2
    both = lax.dot_general(pairs, high, FIRST, preferred_element_type=f32)
    both += lax.dot_general(pairs, low, FIRST, preferred_element_type=f32)
    return both[:n] + both[n:]


def params(mib=10):
    return pltpu.CompilerParams(vmem_limit_bytes=mib << 20)


def cost(*_):
    return pl.CostEstimate(flops=1, bytes_accessed=1, transcendentals=0)


local = pl.BlockSpec(memory_space=pltpu.VMEM)
scalars = pl.BlockSpec(memory_space=pltpu.SMEM)


def whole(shape):
    return pl.BlockSpec(shape, lambda *_: (0,) * len(shape))


def here(n_cols):
    row, col = lax.axis_index("rows"), lax.axis_index("cols")
    steps = n_cols.bit_length() - 1
    segment = 0
    for s in range(steps - 1):
        bit = ((col >> s) ^ (col >> (s + 1))) & 1
        segment = segment | (bit << (steps - 2 - s))
    return row >> 1, row & 1, segment


def cuts(rows):
    ends = [rows * sum(SHARES[: i + 1]) // sum(SHARES) for i in range(len(SHARES))]
    return list(zip([0, *ends], ends))


def resident(x):
    return pltpu.with_memory_space_constraint(x, pltpu.VMEM)


def forward_kernel(chips, begin, end, slots, l_ref, d_ref, r_ref, *refs):
    *outs, buffer, arrived, d, r, pairs, sems = refs
    m = buffer.shape[1]
    chip, core, _ = here(2)
    kept = chips - outs[0].shape[0] if begin == 0 else 0

    def job(n):
        return chips - 1 - (n >> 1), 1 - (n & 1)

    def copy(n):
        t, side = job(n)
        start = pl.multiple_of(((chip ^ t) * 2 + (core ^ side)) * m, m)
        slot = lax.rem(n, slots)
        return pltpu.make_async_copy(l_ref.at[pl.ds(start, m), :], buffer.at[slot], arrived.at[slot])

    copy_d = pltpu.make_async_copy(d_ref, d, sems.at[0])
    copy_r = pltpu.make_async_copy(r_ref, r, sems.at[1])
    copy_d.start()
    for n in range(begin, min(begin + slots - 1, end)):
        copy(n).start()
    copy_r.start()
    copy_d.wait()
    pairs[...] = pair(d[...])

    def step(n, carry):
        @pl.when(n + slots - 1 < end)
        def _():
            copy(n + slots - 1).start()

        copy(n).wait()
        value = wide(buffer[lax.rem(n, slots)], pairs[...])
        t, side = job(n)
        if begin:
            outs[0][t, :m, :] = value
            return carry

        @pl.when(side == 0)
        def _():
            outs[0][t - kept, :m, :] = value

        @pl.when(side == 1)
        def _():
            outs[1][t, :m, :] = value

        return carry

    lax.fori_loop(begin, end, step, 0)
    copy_r.wait()
    norm_now = jnp.sum(r[...] * r[...], axis=0, keepdims=True)
    dir_norm = jnp.sum(d[...] * d[...], axis=0, keepdims=True)
    for ref in outs:
        for t in range(ref.shape[0]):
            ref[t, m:, :] = jnp.zeros((PAD, d.shape[1]), f32)
            ref[t, m : m + 1, :] = norm_now
            ref[t, m + 1 : m + 2, :] = dir_norm


def forward(inv_factor, direction, residual, chips, own):
    n, depth = inv_factor.shape
    t = direction.shape[1]
    m = n // chips // 2
    begin, end = (2 * chips - 1, 2 * chips) if own else (0, 2 * chips - 1)
    out = tuple(
        jax.ShapeDtypeStruct((count, m + PAD, t), f32)
        for count in ((1,) if own else (chips - 1, chips))
    )
    slots = 4
    far = pl.BlockSpec(memory_space=pl.ANY)
    return pl.pallas_call(
        functools.partial(forward_kernel, chips, begin, end, slots),
        in_specs=[far] * 3,
        out_specs=(local,) * len(out),
        out_shape=out,
        scratch_shapes=[
            pltpu.VMEM((slots, m, depth), f32),
            pltpu.SemaphoreType.DMA((slots,)),
            pltpu.VMEM((depth, t), f32),
            pltpu.VMEM((depth, t), f32),
            pltpu.VMEM((depth, 2 * t), bf16),
            pltpu.SemaphoreType.DMA((2,)),
        ],
        compiler_params=params(40),
        cost_estimate=cost(),
    )(*[pltpu.with_memory_space_constraint(x, pltpu.HBM) for x in (inv_factor, direction, residual)])


def add_kernel(n_terms, n_held, *refs):
    terms, outs = refs[:n_terms], refs[n_terms + n_held :]
    if len(outs) > 1 and len(terms[0].shape) == 3:
        outs[0][...] = terms[1][0]
        for i, out in enumerate(outs[1:]):
            out[...] = terms[0][i] + terms[1][i + 1]
        return
    value = terms[0][...]
    for term in terms[1:]:
        value += term[...]
    start = 0
    for out in outs:
        out[...] = value[start : start + out.shape[0], :]
        start += out.shape[0]


def add(terms, shapes, held=()):
    out = tuple(jax.ShapeDtypeStruct(shape, f32) for shape in shapes)
    return pl.pallas_call(
        functools.partial(add_kernel, len(terms), len(held)),
        in_specs=[local] * (len(terms) + len(held)),
        out_specs=(local,) * len(out),
        out_shape=out,
        compiler_params=params(),
        cost_estimate=cost(),
    )(*terms, *map(resident, held))


def cut_kernel(begin, x_ref, *refs):
    refs[-1][...] = x_ref[begin : begin + refs[-1].shape[0], :]


def cut(x, begin, rows, held=()):
    return pl.pallas_call(
        functools.partial(cut_kernel, begin),
        in_specs=[local] * (1 + len(held)),
        out_specs=local,
        out_shape=jax.ShapeDtypeStruct((rows, x.shape[1]), f32),
        compiler_params=params(),
        cost_estimate=cost(),
    )(x, *map(resident, held))


def kernel_kernel(segments, place, own_ref, other_ref, c_ref, high_ref, low_ref, ph, plo, psq):
    @pl.when(pl.program_id(0) == 0)
    def _():
        n = own_ref.shape[0]
        seg = n // segments
        for side, ref in enumerate((own_ref, other_ref)):
            for u in range(segments):
                start = pl.multiple_of((place[2] ^ u) * seg, seg)
                p = ref[pl.ds(start, seg), :]
                at = slice(side * n + u * seg, side * n + (u + 1) * seg)
                ph[at, :], plo[at, :] = split(p)
                psq[at, :] = jnp.broadcast_to(0.5 * jnp.sum(p * p, axis=1, keepdims=True), (seg, 128))

    c = c_ref[...]
    ch, cl = split(c)
    x = lax.dot_general(ch, ph[...], LAST, preferred_element_type=f32)
    x += lax.dot_general(ch, plo[...], LAST, preferred_element_type=f32)
    x += lax.dot_general(cl, ph[...], LAST, preferred_element_type=f32)
    center_sq = 0.5 * jnp.sum(c * c, axis=1, keepdims=True)
    point_sq = psq[...].T[0:1, :]
    high_ref[0], low_ref[0] = split(jnp.exp(x - (center_sq + point_sq)))


def gaussian(place, own, other, centers, chips, segments):
    n, width = own.shape
    m = centers.shape[0] // chips // 2
    out = jax.ShapeDtypeStruct((chips, m, 2 * n), bf16)
    block = pl.BlockSpec((1, m, 2 * n), lambda i, s: (i, 0, 0))
    return pl.pallas_call(
        functools.partial(kernel_kernel, segments),
        grid_spec=pltpu.PrefetchScalarGridSpec(
            num_scalar_prefetch=1,
            grid=(chips,),
            in_specs=[
                whole((n, width)),
                whole((n, width)),
                pl.BlockSpec((m, width), lambda i, s: (2 * (s[0] ^ i) + s[1], 0)),
            ],
            out_specs=(block, block),
            scratch_shapes=[
                pltpu.VMEM((2 * n, width), bf16),
                pltpu.VMEM((2 * n, width), bf16),
                pltpu.VMEM((2 * n, 128), f32),
            ],
        ),
        out_shape=(out, out),
        compiler_params=params(),
        cost_estimate=cost(12 * chips * m * n * width, 8 * chips * m * n, 2 * chips * m * n),
    )(place, own, other, pltpu.with_memory_space_constraint(centers, pltpu.HBM))


def predict_kernel(shift, begin, first, last, high_ref, low_ref, piece_ref, *refs):
    rows = slice(begin, begin + piece_ref.shape[0])
    value = turned(pair(piece_ref[...]), high_ref[shift, rows, :], low_ref[shift, rows, :])
    if not first:
        value += refs[0][...]
    if last:
        half = value.shape[1] // 2
        refs[-2][...] = value[:, :half].T
        refs[-1][...] = value[:, half:].T
    else:
        refs[-1][...] = value


def predict(shift, begin, high, low, piece, acc, last):
    _, m, n = high.shape
    t = piece.shape[1]
    args = [resident(high), resident(low), piece] + ([] if acc is None else [acc])
    if last:
        out = (jax.ShapeDtypeStruct((n // 2, t), f32),) * 2
    else:
        out = jax.ShapeDtypeStruct((t, n), f32)
    return pl.pallas_call(
        functools.partial(predict_kernel, shift, begin, acc is None, last),
        in_specs=[local] * len(args),
        out_specs=(local,) * 2 if last else local,
        out_shape=out,
        compiler_params=params(),
        cost_estimate=cost(8 * m * n * t, 4 * m * n),
    )(*args)


def back_kernel(shifts, last, high_ref, low_ref, own_ref, *refs):
    half, n = own_ref.shape
    m = high_ref.shape[1]
    outs = refs[-len(shifts) :]
    begin = half if last else 0
    pairs = pair(refs[0][...] if last else own_ref[...])
    if last:
        norm = sum(
            jnp.sum(ref[...] * ref[...], axis=0, keepdims=True) for ref in (own_ref, refs[0])
        )
    for i, (shift, out_ref) in enumerate(zip(shifts, outs)):
        both = jnp.dot(high_ref[shift, :, begin : begin + half], pairs, preferred_element_type=f32)
        both += jnp.dot(low_ref[shift, :, begin : begin + half], pairs, preferred_element_type=f32)
        value = both[:, :n] + both[:, n:]
        if last:
            value += refs[1 + i][...]
            out_ref[m:, :] = jnp.zeros((PAD, n), f32)
            out_ref[m : m + 1, :] = norm
        out_ref[:m, :] = value


def back_product(shifts, high, low, own, other=None, before=(), held=()):
    m = high.shape[1]
    t = own.shape[1]
    last = other is not None
    args = [resident(high), resident(low), own, *([other] if last else []), *before]
    args += map(resident, held)
    out = (jax.ShapeDtypeStruct((m + PAD if last else m, t), f32),) * len(shifts)
    return pl.pallas_call(
        functools.partial(back_kernel, shifts, last),
        in_specs=[local] * len(args),
        out_specs=(local,) * len(out),
        out_shape=out,
        compiler_params=params(),
        cost_estimate=cost(),
    )(*args)


def transposed_kernel(m, places, first, l_ref, *refs):
    chip, core, _ = here(2)
    pieces, refs = refs[: len(places)], refs[len(places) :]
    value = None if first else refs[0][...]
    for (shift, begin, side), ref in zip(places, pieces):
        n = ref.shape[0]
        step = min(n, 512)
        for i in range(0, n, step):
            start = pl.multiple_of(((chip ^ shift) * 2 + (core ^ side)) * m + begin + i, step)
            high, low = split(l_ref[pl.ds(start, step), :])
            share = turned(pair(ref[i : i + step, :]), high, low)
            value = share if value is None else value + share
    refs[-1][...] = value


def transposed(m, places, inv_factor, pieces, acc):
    depth = inv_factor.shape[1]
    t = pieces[0].shape[1]
    args = [resident(inv_factor), *pieces] + ([] if acc is None else [acc])
    return pl.pallas_call(
        functools.partial(transposed_kernel, m, places, acc is None),
        in_specs=[local] * len(args),
        out_specs=local,
        out_shape=jax.ShapeDtypeStruct((t, depth), f32),
        compiler_params=params(),
        cost_estimate=cost(),
    )(*args)


def last_kernel(m, places, part, segments, l_ref, acc_ref, *refs):
    pieces, (keep_ref, send_ref, image) = refs[: len(places)], refs[len(places) :]
    chip, core, segment = here(2 * segments)
    depth = acc_ref.shape[1]
    seg, n = depth // segments, image.shape[1]
    begin, end = cuts(seg)[part]
    bands = [(u * seg + begin, u * seg + end) for u in range(segments)]
    apart = all(edge % 128 == 0 for band in bands for edge in band)
    pairs = [pair(ref[...]) for ref in pieces]
    for u, (low_edge, high_edge) in enumerate(bands if apart else [(0, depth)]):
        value = acc_ref[:, low_edge:high_edge]
        for (shift, first), values in zip(places, pairs):
            count = values.shape[0]
            start = pl.multiple_of(((chip ^ shift) * 2 + 1 - core) * m + first, count)
            high, low = split(l_ref[pl.ds(start, count), low_edge:high_edge])
            value += turned(values, high, low)
        value = value.T
        if apart:
            image[u] = value
        else:
            for i, (first, final) in enumerate(bands):
                image[i] = value[first:final, :]
    half = segments // 2
    for u in range(segments):
        ref = keep_ref if u < half else send_ref
        ref[(u % half) * n : (u % half + 1) * n, :] = image[segment ^ u]


def last_transposed(m, part, segments, inv_factor, pieces, acc):
    t, depth = acc.shape
    begin, end = cuts(depth // segments)[part]
    out = jax.ShapeDtypeStruct((segments // 2 * (end - begin), t), f32)
    args = [resident(inv_factor), acc, *[piece for _, _, piece in pieces]]
    return pl.pallas_call(
        functools.partial(last_kernel, m, [piece[:2] for piece in pieces], part, segments),
        in_specs=[local] * len(args),
        out_specs=(local, local),
        out_shape=(out, out),
        scratch_shapes=[pltpu.VMEM((segments, end - begin, t), f32)],
        compiler_params=params(),
        cost_estimate=cost(),
    )(*args)


def update_kernel(begin, rows, segments, image_ref, r_ref, d_ref, pred_ref, norm_ref, *refs):
    new_ref, sum_ref = refs[-2:]
    norm_now, dir_norm = norm_ref[0:1, :], norm_ref[1:2, :]
    curvature = pred_ref[0:1, :] + ridge_weight * dir_norm
    step = norm_now / curvature
    start = here(2 * segments)[2] * rows + begin
    at = pl.ds(pl.multiple_of(start, PAD), image_ref.shape[0])
    new = r_ref[at, :] - step * (image_ref[...] + ridge_weight * d_ref[at, :])
    new_ref[...] = new
    total = jnp.broadcast_to(jnp.sum(new * new, axis=0, keepdims=True), sum_ref.shape)
    if len(refs) == 3:
        total += refs[0][...]
    sum_ref[...] = total


def update(begin, image, residual, direction, pred_norm, norms, before, segments):
    rows = residual.shape[0] // segments
    args = [image, residual, direction, pred_norm, norms] + ([] if before is None else [before])
    out = (jax.ShapeDtypeStruct(image.shape, f32), jax.ShapeDtypeStruct(norms.shape, f32))
    return pl.pallas_call(
        functools.partial(update_kernel, begin, rows, segments),
        in_specs=[local] * len(args),
        out_specs=(local, local),
        out_shape=out,
        compiler_params=params(),
        cost_estimate=cost(),
    )(*args)


def finish_kernel(segments, n_pieces, *refs):
    pieces = refs[:n_pieces]
    d_ref, norm_ref, next_ref, res_ref, dir_ref, new, sems = refs[n_pieces:]
    segment = here(2 * segments)[2]
    seg = d_ref.shape[0] // segments
    each = n_pieces // len(SHARES)
    places = []
    for c, (begin, end) in enumerate(cuts(seg)):
        u, n = 0, end - begin
        for piece in pieces[c * each : (c + 1) * each]:
            for j in range(piece.shape[0] // n):
                at = pl.ds(pl.multiple_of((segment ^ u) * seg + begin, PAD), n)
                places.append((piece.at[pl.ds(j * n, n), :], at))
                u += 1
    residuals = [
        pltpu.make_async_copy(rows, res_ref.at[at, :], sems.at[0, i])
        for i, (rows, at) in enumerate(places)
    ]
    directions = [
        pltpu.make_async_copy(new.at[at, :], dir_ref.at[at, :], sems.at[1, i])
        for i, (_, at) in enumerate(places)
    ]
    for copy in residuals:
        copy.start()
    ratio = next_ref[0:1, :] / norm_ref[0:1, :]
    for (rows, at), copy in zip(places, directions):
        new[at, :] = rows[...] + ratio * d_ref[at, :]
        copy.start()
    for copy in residuals + directions:
        copy.wait()


def finish(pieces, direction, norms, norm_next, segments):
    out = jax.ShapeDtypeStruct(direction.shape, f32)
    args = [*pieces, direction, norms, norm_next]
    far = pl.BlockSpec(memory_space=pl.ANY)
    return pl.pallas_call(
        functools.partial(finish_kernel, segments, len(pieces)),
        in_specs=[local] * len(args),
        out_specs=(far, far),
        out_shape=(out, out),
        scratch_shapes=[
            pltpu.VMEM(direction.shape, f32),
            pltpu.SemaphoreType.DMA((2, segments * len(SHARES))),
        ],
        compiler_params=params(),
        cost_estimate=cost(),
    )(*args)


def body(n_rows, n_cols, points, centers, inv_factor, solution, residual, direction):
    chips = n_rows // 2
    steps = n_cols.bit_length() - 1
    masks = [(2 << s) - 1 for s in range(steps)]
    halving, last_mask = masks[:-1], masks[-1]
    segments = n_cols // 2

    def swap(x, axis, mask):
        size = n_rows if axis == "rows" else n_cols
        return lax.ppermute(x, axis, [(i, i ^ mask) for i in range(size)])

    place = jnp.stack(here(n_cols)).astype(jnp.int32)
    order = list(range(1, chips))

    def gather(own, held=(), first=()):
        if chips != 4:
            return first, [(i, 0, swap(own, "rows", 2 * i)) for i in order]
        half = own.shape[0] // 2
        x, y = swap(own, "rows", 2), swap(own, "rows", 4)
        x, first = lax.optimization_barrier((x, first))
        through_y = swap(cut(x, half, half, held), "rows", 4)
        through_x = swap(cut(y, 0, half, held), "rows", 2)
        return first, [(1, 0, x), (2, 0, y), (3, half, through_y), (3, 0, through_x)]

    other_points = swap(points, "rows", 1)
    keep, send = forward(inv_factor, direction, residual, chips, False)
    m, t = send.shape[1] - PAD, send.shape[2]
    part, *totals = add([keep, swap(send, "rows", 1)], [(m + PAD, t)] * chips)
    got = [swap(totals[i - 1], "rows", 2 * i) for i in order]
    direction, part = lax.optimization_barrier((direction, part))
    (keep,) = forward(inv_factor, direction, residual, chips, True)
    mapped, norms = add([keep[0], part, *got], [(m, t), (PAD, t)])
    high, low = gaussian(place, points, other_points, centers, chips, segments)
    mapped, high, low = lax.optimization_barrier((mapped, high, low))

    arrived = [(0, 0, mapped), *gather(mapped)[1]]
    acc = None
    for j, (shift, begin, piece) in enumerate(arrived):
        acc = predict(shift, begin, high, low, piece, acc, j == len(arrived) - 1)
    keep, send = acc
    part = keep + swap(send, "rows", 1)
    for mask in halving:
        half = part.shape[0] // 2
        part = part[:half] + swap(part[half:], "cols", mask)
    part = part + swap(part, "cols", last_mask)
    for mask in halving[::-1]:
        part = jnp.concatenate([part, swap(part, "cols", mask)], axis=0)
    before = back_product((*order, 0), high, low, part)
    other = swap(part, "rows", 1)
    pieces = back_product(order, high, low, part, other, before[:-1])
    got = [swap(piece, "rows", 2 * i) for i, piece in zip(order, pieces)]
    got += back_product((0,), high, low, part, other, before[-1:], (inv_factor,))
    own, pred_norm = add([got[-1], *got[:-1]], [(m, t), (PAD, t)], (inv_factor,))

    acc = transposed(m, [(0, 0, 0), (0, 0, 1)], inv_factor, [own, swap(own, "rows", 1)], None)
    acc, arrived = gather(own, (inv_factor,), acc)
    late = []
    turns = [arrived[:2], *([one] for one in arrived[2:])]
    for turn in turns:
        pieces, acc = lax.optimization_barrier(([one[2] for one in turn], acc))
        places = [(shift, begin, 0) for shift, begin, _ in turn]
        late += [(*one[:2], swap(piece, "rows", 1)) for one, piece in zip(turn, pieces)]
        acc = transposed(m, places, inv_factor, pieces, acc)
    pieces, norm_next, step_one, step_two, done = [], None, (), (), ()
    for c, (begin, _) in enumerate(cuts(residual.shape[0] // segments)):
        image, send = last_transposed(m, c, segments, inv_factor, late, acc)
        send, step_one = lax.optimization_barrier((send, step_one))
        step_one = swap(send, "cols", masks[0])
        image = image + step_one
        for mask in halving[1:]:
            half = image.shape[0] // 2
            image = image[:half] + swap(image[half:], "cols", mask)
        image, step_two = lax.optimization_barrier((image, step_two))
        step_two = swap(image, "cols", last_mask)
        image = image + step_two
        image, done = lax.optimization_barrier((image, done))
        new, norm_next = update(
            begin, image, residual, direction, pred_norm, norms, norm_next, segments
        )
        pieces.append(new)
        for mask in halving[::-1]:
            done = swap(new, "cols", mask)
            pieces.append(done)
            new = jnp.concatenate([new, done], axis=0)
    for mask in halving[::-1]:
        norm_next = norm_next + swap(norm_next, "cols", mask)
    norm_next = jnp.sum(lax.all_gather(norm_next, "rows"), axis=0)
    step = norms[0:1] / (pred_norm[0:1] + ridge_weight * norms[1:2])
    new_solution = solution + step * direction
    new_residual, new_direction = finish(
        pieces, direction, norms, norm_next, segments
    )
    return new_solution, new_residual, new_direction


def solution(mesh):
    return jax.shard_map(
        functools.partial(body, mesh.shape["rows"], mesh.shape["cols"]),
        mesh=mesh,
        in_specs=(
            P("rows", None),
            P("cols", None),
            P("cols", "rows"),
            P("rows", None),
            P("rows", None),
            P("rows", None),
        ),
        out_specs=(P("rows", None), P("rows", None), P("rows", None)),
        check_vma=False,
    )
```
